256 devices in a mesh: row: 16 (over x, z_lo, core), col: 16 (over y, z_hi).
Axes of the slice: x: 4, y: 4, z: 8 (z_hi: 4, z_lo: 2; z = z_hi * 2 + z_lo), core: 2. Of those that a mesh axis runs over, the one named last changes fastest.
Arguments:
- sequence_features: bfloat16 [1280, 64, 128], P(('row', 'col')), may hold values from -6 to 6
- first_projection: bfloat16 [64, 32], replicated, may hold values from -0.75 to 0.75
- second_projection: bfloat16 [64, 32], replicated, may hold values from -0.75 to 0.75
- final_projection: bfloat16 [1024, 128], replicated, may hold values from -0.1875 to 0.1875
- final_offset: float32 [128], replicated, may hold values from -3 to 3
- edge_change_cotangent: bfloat16 [1280, 1280, 128], P('row', 'col'), may hold values from -6 to 6
Outputs:
- pair_delta: bfloat16 [1280, 1280, 128], P('row', 'col')
- alignment_gradient: float32 [1280, 64, 128], P(('row', 'col'))
- left_weight_gradient: float32 [64, 32], replicated
- right_weight_gradient: float32 [64, 32], replicated
- output_weight_gradient: float32 [1024, 128], replicated
- bias_gradient: float32 [128], replicated
The draws below stay inside these ranges and needn't reach their ends.
All inputs are finite; a program needn't handle non-finite values.
Results may differ from the reference program's by a relative error of at most 0.022.
Values may be sent and summed in bfloat16 or wider, within the bound.
No kernel may reach another device: no remote copies, remote signals or barrier semaphores. Data moves between devices by JAX's collectives and lax.ppermute only.
A program may use at most 64 MiB of HBM per device.

```python
import math
import jax
import jax.numpy as jnp
from jax import lax

FACTOR_WIDTH = 32
FEATURE_DEPTH = 64
EDGE_FEATURES = 128
SEQUENCE_NUMBER = 128
CHAIN_LENGTH = 1280


def level_of(stream_key, extent, pieces, least, high):
    gain = 1.0
    for position, shards_of in pieces:
        steps = jax.random.uniform(jax.random.fold_in(jax.random.fold_in(stream_key, 6), position), (shards_of,), jnp.float32, least / len(pieces), high / len(pieces))
        gain = gain * jnp.repeat(jnp.exp(steps), extent[position] // shards_of).reshape((-1,) + (1,) * (len(extent) - 1 - position))
    return gain


def gaussian(stream_key, shape, scale, reach, split=(), held_as=jnp.bfloat16):
    loudness = level_of(stream_key, shape, split, -0.22, 0.18) if split else 1.0
    values = jax.random.normal(stream_key, shape, jnp.float32) * scale * loudness
    return jnp.minimum(jnp.maximum(values, -reach), reach).astype(held_as)


def setup_inputs(seed: int = 0) -> dict:
    keys = jax.random.split(jax.random.key(seed), 7)
    sequence_features = gaussian(keys[0], (CHAIN_LENGTH, FEATURE_DEPTH, SEQUENCE_NUMBER), 1.0, 6.0, ((0, 256),))
    first_projection = gaussian(keys[1], (FEATURE_DEPTH, FACTOR_WIDTH), FEATURE_DEPTH ** -0.5, 0.75)
    second_projection = gaussian(keys[2], (FEATURE_DEPTH, FACTOR_WIDTH), FEATURE_DEPTH ** -0.5, 0.75)
    final_projection = gaussian(keys[3], (FACTOR_WIDTH * FACTOR_WIDTH, EDGE_FEATURES), (FACTOR_WIDTH * FACTOR_WIDTH) ** -0.5, 0.1875)
    final_offset = gaussian(keys[4], (EDGE_FEATURES,), 0.5, 3.0, (), jnp.float32)
    edge_change_cotangent = gaussian(keys[5], (CHAIN_LENGTH, CHAIN_LENGTH, EDGE_FEATURES), 1.0, 6.0, ((0, 16), (1, 16)))
    return dict(sequence_features=sequence_features, first_projection=first_projection, second_projection=second_projection, final_projection=final_projection, final_offset=final_offset, edge_change_cotangent=edge_change_cotangent)


def reference(sequence_features, first_projection, second_projection, final_projection, final_offset, edge_change_cotangent):
    single_number = jnp.float32
    sequences_single = sequence_features.astype(single_number)
    left_float = first_projection.astype(single_number)
    right_float = second_projection.astype(single_number)
    first_factors = jnp.einsum('ket,ei->kit', sequences_single, left_float).astype(jnp.bfloat16)
    right_values = jnp.einsum('ket,ei->kit', sequences_single, right_float).astype(jnp.bfloat16)
    reciprocal_sequences = 1.0 / SEQUENCE_NUMBER
    edge_tile = math.gcd(CHAIN_LENGTH, 16)
    overall_number = CHAIN_LENGTH // edge_tile
    right_wide = right_values.astype(single_number)

    def one_block(carry, arguments):
        grad_out_acc, right_acc = carry
        left_blk, tangent = arguments
        left_broad = left_blk.astype(single_number)
        outer = jnp.einsum('ics,jds->ijcd', left_broad, right_wide)
        outer = (outer * reciprocal_sequences).astype(jnp.bfloat16)
        flat = outer.reshape(edge_tile * CHAIN_LENGTH, FACTOR_WIDTH * FACTOR_WIDTH)
        pair = jnp.dot(flat, final_projection, preferred_element_type=single_number) + final_offset
        tangent_flat = tangent.reshape(edge_tile * CHAIN_LENGTH, EDGE_FEATURES)
        outer_grad = jnp.dot(tangent_flat, final_projection.T, preferred_element_type=single_number).astype(jnp.bfloat16)
        grad_out_acc = grad_out_acc + jnp.dot(flat.T, tangent_flat, preferred_element_type=single_number)
        outer_grad = outer_grad.reshape(edge_tile, CHAIN_LENGTH, FACTOR_WIDTH, FACTOR_WIDTH).astype(single_number)
        first_factor_cotangent = jnp.einsum('ijcd,jds->ics', outer_grad, right_wide) * reciprocal_sequences
        right_acc = right_acc + jnp.einsum('ijcd,ics->jds', outer_grad, left_broad)
        return (grad_out_acc, right_acc), (pair.astype(jnp.bfloat16).reshape(edge_tile, CHAIN_LENGTH, EDGE_FEATURES), first_factor_cotangent)

    beginning_offset = (jnp.zeros((FACTOR_WIDTH * FACTOR_WIDTH, EDGE_FEATURES), single_number), jnp.zeros((CHAIN_LENGTH, FACTOR_WIDTH, SEQUENCE_NUMBER), single_number))
    arguments = (first_factors.reshape(overall_number, edge_tile, FACTOR_WIDTH, SEQUENCE_NUMBER), edge_change_cotangent.reshape(overall_number, edge_tile, CHAIN_LENGTH, EDGE_FEATURES))
    (grad_out_acc, right_acc), (pairs, first_cotangent_pieces) = lax.scan(one_block, beginning_offset, arguments)
    pair_delta = pairs.reshape(CHAIN_LENGTH, CHAIN_LENGTH, EDGE_FEATURES)
    first_factor_cotangent = first_cotangent_pieces.reshape(CHAIN_LENGTH, FACTOR_WIDTH, SEQUENCE_NUMBER)
    right_gradient = right_acc * reciprocal_sequences
    upper_precision = lax.Precision.HIGHEST
    alignment_gradient = jnp.einsum('awr,iw->air', first_factor_cotangent, left_float, precision=upper_precision) + jnp.einsum('awr,iw->air', right_gradient, right_float, precision=upper_precision)
    inverse_residues = 1.0 / CHAIN_LENGTH
    left_weight_gradient = jnp.einsum('gph,gah->pa', sequences_single, first_factor_cotangent, precision=upper_precision) * inverse_residues
    right_weight_gradient = jnp.einsum('gph,gah->pa', sequences_single, right_gradient, precision=upper_precision) * inverse_residues
    output_weight_gradient = grad_out_acc * inverse_residues
    bias_gradient = jnp.sum(edge_change_cotangent.astype(single_number), axis=(0, 1)) * inverse_residues
    return (pair_delta, alignment_gradient, left_weight_gradient, right_weight_gradient, output_weight_gradient, bias_gradient)
```

```python
import functools

import jax
import jax.numpy as jnp
from jax import lax
from jax.experimental import pallas as pl
from jax.experimental.pallas import tpu as pltpu
from jax.sharding import PartitionSpec as P

BF = jnp.bfloat16
F32 = jnp.float32
LANES = 128
VMEM = 56 * 1024 * 1024


def shift(x, axis, stride, size, k):
    n = lax.axis_size(axis)
    perm = []
    for i in range(n):
        digit = (i // stride) % size
        perm.append((i, i + stride * ((digit + k) % size - digit)))
    return lax.ppermute(x, axis, perm)


def digit_of(axis, stride, size):
    return lax.rem(lax.axis_index(axis) // stride, size)


def gather_digit(x, axis, stride, size):
    me = digit_of(axis, stride, size)
    parts = [x] + [shift(x, axis, stride, size, k) for k in range(1, size)]
    back = parts[::-1]
    ring = jnp.stack(back + back[:-1])
    return lax.dynamic_slice_in_dim(ring, size - 1 - me, size, 0)


def scatter_digit(x, axis, stride, size, link):
    me = digit_of(axis, stride, size)
    total = lax.dynamic_index_in_dim(x, me, 0, keepdims=False)
    for k in range(1, size):
        block = lax.dynamic_index_in_dim(x, lax.rem(me + k, size), 0, keepdims=False)
        total = total + shift(block.astype(link), axis, stride, size, k).astype(F32)
    return total


def sum_digit(x, axis, stride, size):
    total = x
    for k in range(1, size):
        total = total + shift(x, axis, stride, size, k)
    return total


def swap_axes(x):
    n = lax.axis_size("row")
    return lax.ppermute(
        x, ("row", "col"), [(r * n + c, c * n + r) for r in range(n) for c in range(n)]
    )


def project(source, weight):
    return jnp.einsum("ket,ei->kit", source, weight, preferred_element_type=F32).astype(BF)


def padded_rows(t, rows):
    return jnp.concatenate([t, jnp.zeros((rows - t.shape[0], t.shape[1]), t.dtype)], axis=0)


def outer_grad_kernel(width, group, t_ref, w_ref, g_ref, bias_ref):
    @pl.when(pl.program_id(0) == 0)
    def _():
        bias_ref[...] = jnp.zeros_like(bias_ref)

    channels = w_ref.shape[0]
    total = jnp.zeros((1, LANES), F32)
    for pair in range(group // 2):
        a, b = t_ref[2 * pair], t_ref[2 * pair + 1]
        total = total + jnp.sum(a.astype(F32) + b.astype(F32), axis=0, keepdims=True)
        both = jnp.concatenate([padded_rows(a, LANES), padded_rows(b, LANES)], axis=0)
        grad = lax.dot_general(
            w_ref[...], both, (((1,), (1,)), ((), ())), preferred_element_type=F32
        ).astype(BF)
        for half in range(2):
            row = (2 * pair + half) * width
            for d in range(channels // width):
                g_ref[pl.ds(row, width), pl.ds(d * LANES, LANES)] = grad[
                    d * width : (d + 1) * width, half * LANES : (half + 1) * LANES
                ]
    bias_ref[...] += jnp.broadcast_to(total, bias_ref.shape)


def factor_grad_kernel(width, scale, steps, l_ref, r_ref, g_ref, gl_ref, gr_ref, acc_ref):
    step = pl.program_id(0)

    @pl.when(step == 0)
    def _():
        acc_ref[...] = jnp.zeros_like(acc_ref)

    grad = g_ref[...]
    gl_ref[...] = (jnp.dot(grad, r_ref[...], preferred_element_type=F32) * scale).astype(
        gl_ref.dtype
    )
    lt = l_ref[...].T
    chunk = 512
    for n in range(acc_ref.shape[1] // chunk):
        part = pl.ds(n * chunk, chunk)
        acc_ref[:, part] += jnp.dot(lt, g_ref[:, part], preferred_element_type=F32)

    @pl.when(step == steps - 1)
    def _():
        columns = gr_ref.shape[1]
        for d in range(gr_ref.shape[0]):
            block = acc_ref[:, d * LANES : (d + 1) * LANES].T
            gr_ref[d] = block[:columns].astype(gr_ref.dtype)


def pair_kernel(
    width, group, l_ref, r_ref, t_ref, wt_ref, off_ref, p_ref, gw_ref, rt_ref, outer_ref
):
    columns = t_ref.shape[1]
    depth = r_ref.shape[0] // LANES

    @pl.when(pl.program_id(0) == 0)
    def _():
        gw_ref[...] = jnp.zeros_like(gw_ref)
        for d in range(depth):
            part = pl.ds(d * LANES, LANES)
            rt_ref[:, part] = r_ref[part, :].T

    per = 4
    for n in range(depth // per):
        block = jnp.dot(
            l_ref[...], rt_ref[:, pl.ds(n * per * LANES, per * LANES)], preferred_element_type=F32
        ).astype(BF)
        for i in range(group):
            for d in range(per):
                outer_ref[
                    i // 2,
                    pl.ds((n * per + d) * width, width),
                    pl.ds((i % 2) * LANES, LANES),
                ] = block[i * width : (i + 1) * width, d * LANES : (d + 1) * LANES]
    offset = off_ref[...]
    for pair in range(group // 2):
        outer = outer_ref[pair]
        out = jnp.dot(wt_ref[...], outer, preferred_element_type=F32).T
        p_ref[2 * pair] = (out[:columns] + offset).astype(BF)
        p_ref[2 * pair + 1] = (out[LANES : LANES + columns] + offset).astype(BF)
        both = jnp.concatenate(
            [padded_rows(t_ref[2 * pair], LANES), padded_rows(t_ref[2 * pair + 1], LANES)], axis=0
        )
        gw_ref[...] += jnp.dot(outer, both, preferred_element_type=F32)


def params():
    return pltpu.CompilerParams(
        dimension_semantics=("arbitrary",), vmem_limit_bytes=VMEM
    )


def outer_grads(cotangent, weight, width):
    rows, columns, out = cotangent.shape
    group = 8
    channels = weight.shape[0]
    depth = channels // width
    return pl.pallas_call(
        functools.partial(outer_grad_kernel, width, group),
        grid=(rows // group,),
        in_specs=[
            pl.BlockSpec((group, columns, out), lambda i: (i, 0, 0)),
            pl.BlockSpec((channels, out), lambda i: (0, 0)),
        ],
        out_specs=[
            pl.BlockSpec((group * width, depth * LANES), lambda i: (i, 0)),
            pl.BlockSpec((8, out), lambda i: (0, 0)),
        ],
        out_shape=[
            jax.ShapeDtypeStruct((rows * width, depth * LANES), BF),
            jax.ShapeDtypeStruct((8, out), F32),
        ],
        compiler_params=params(),
        cost_estimate=pl.CostEstimate(
            flops=4 * rows * columns * channels * out, bytes_accessed=22 << 20, transcendentals=0
        ),
        name="outer_grads",
    )(cotangent, weight)


def factor_grads(left, right, grad, width, columns, scale):
    rows, sequences = left.shape
    depth = right.shape[0] // LANES
    block = 512
    steps = rows // block
    return pl.pallas_call(
        functools.partial(factor_grad_kernel, width, scale, steps),
        grid=(steps,),
        in_specs=[
            pl.BlockSpec((block, sequences), lambda i: (i, 0)),
            pl.BlockSpec(right.shape, lambda i: (0, 0)),
            pl.BlockSpec((block, depth * LANES), lambda i: (i, 0)),
        ],
        out_specs=[
            pl.BlockSpec((block, sequences), lambda i: (i, 0)),
            pl.BlockSpec((depth, columns, sequences), lambda i: (0, 0, 0)),
        ],
        out_shape=[
            jax.ShapeDtypeStruct((rows, sequences), F32),
            jax.ShapeDtypeStruct((depth, columns, sequences), F32),
        ],
        scratch_shapes=[pltpu.VMEM((sequences, depth * LANES), F32)],
        compiler_params=params(),
        cost_estimate=pl.CostEstimate(
            flops=8 * rows * depth * LANES * sequences, bytes_accessed=24 << 20, transcendentals=0
        ),
        name="factor_grads",
    )(left, right, grad)


def pairs(left, right, cotangent, weight_t, offset, width):
    rows, columns, out = cotangent.shape
    sequences = left.shape[1]
    channels = weight_t.shape[1]
    group = 8
    depth = right.shape[0] // LANES
    return pl.pallas_call(
        functools.partial(pair_kernel, width, group),
        grid=(rows // group,),
        in_specs=[
            pl.BlockSpec((group * width, sequences), lambda i: (i, 0)),
            pl.BlockSpec(right.shape, lambda i: (0, 0)),
            pl.BlockSpec((group, columns, out), lambda i: (i, 0, 0)),
            pl.BlockSpec((out, channels), lambda i: (0, 0)),
            pl.BlockSpec((1, out), lambda i: (0, 0)),
        ],
        out_specs=[
            pl.BlockSpec((group, columns, out), lambda i: (i, 0, 0)),
            pl.BlockSpec((channels, out), lambda i: (0, 0)),
        ],
        out_shape=[
            jax.ShapeDtypeStruct((rows, columns, out), BF),
            jax.ShapeDtypeStruct((channels, out), F32),
        ],
        scratch_shapes=[
            pltpu.VMEM((sequences, depth * LANES), BF),
            pltpu.VMEM((group // 2, channels, 2 * LANES), BF),
        ],
        compiler_params=params(),
        cost_estimate=pl.CostEstimate(
            flops=12 * rows * LANES * channels * out, bytes_accessed=6 << 20, transcendentals=0
        ),
        name="pairs",
    )(left, right, cotangent, weight_t, offset)


def shards(
    sequence_features,
    first_projection,
    second_projection,
    final_projection,
    final_offset,
    edge_change_cotangent,
):
    n_row = lax.axis_size("row")
    n_col = lax.axis_size("col")
    owned, _, sequences = sequence_features.shape
    rows, columns, out = edge_change_cotangent.shape
    width = first_projection.shape[1]
    scale = 1.0 / sequences

    weight = final_projection.reshape(width, width, out).swapaxes(0, 1).reshape(-1, out)
    grad, bias_local = outer_grads(edge_change_cotangent, weight, width)

    right = swap_axes(project(sequence_features, second_projection))
    left = project(sequence_features, first_projection) * jnp.asarray(scale, BF)

    left = gather_digit(left, "col", 1, 4)
    left = gather_digit(left, "col", 4, 4)
    left = left.reshape(rows * width, sequences)

    right = gather_digit(right, "row", 2, 2)
    right = gather_digit(right, "row", 4, 4)
    right = gather_digit(right, "row", 1, 2)
    right = right.transpose(4, 1, 2, 0, 3, 5).reshape(width, columns, sequences)
    right = jnp.pad(right, ((0, 0), (0, LANES - columns), (0, 0))).reshape(-1, sequences)

    left_part, right_part = factor_grads(left, right, grad, width, columns, scale)

    left_sum = left_part.reshape(4, 4, owned, width, sequences)
    left_sum = scatter_digit(left_sum, "col", 4, 4, BF)
    left_sum = scatter_digit(left_sum, "col", 1, 4, BF)

    right_sum = right_part.reshape(width, 4, 2, 2, owned, sequences).transpose(3, 1, 2, 4, 0, 5)
    right_sum = scatter_digit(right_sum, "row", 1, 2, BF)
    right_sum = scatter_digit(right_sum, "row", 4, 4, BF)
    right_sum = scatter_digit(right_sum, "row", 2, 2, BF)
    right_sum = swap_axes(right_sum)

    pair_delta, weight_part = pairs(
        left, right, edge_change_cotangent, weight.T, final_offset.reshape(1, out), width
    )

    channels = weight.shape[0]
    total = scatter_digit(weight_part.reshape(2, channels // 2, out), "row", 1, 2, BF)
    total = scatter_digit(total.reshape(4, channels // 8, out), "row", 4, 4, BF)
    total = scatter_digit(total.reshape(2, channels // 16, out), "row", 2, 2, F32)
    total = scatter_digit(total.reshape(4, channels // 64, out), "col", 4, 4, F32)
    total = scatter_digit(total.reshape(4, channels // 256, out), "col", 1, 4, F32)
    total = gather_digit(total, "col", 1, 4).reshape(channels // 64, out)
    total = gather_digit(total, "col", 4, 4).reshape(channels // 16, out)
    total = gather_digit(total, "row", 2, 2).reshape(channels // 8, out)
    total = gather_digit(total, "row", 4, 4).reshape(channels // 2, out)
    total = gather_digit(total, "row", 1, 2).reshape(channels, out)
    total = total.reshape(width, width, out).swapaxes(0, 1).reshape(channels, out)

    exact = lax.Precision.HIGHEST
    wide = sequence_features.astype(F32)
    alignment_gradient = jnp.einsum(
        "awr,iw->air", left_sum, first_projection.astype(F32), precision=exact
    ) + jnp.einsum("awr,iw->air", right_sum, second_projection.astype(F32), precision=exact)
    left_weight = jnp.einsum("gph,gah->pa", wide, left_sum, precision=exact)
    right_weight = jnp.einsum("gph,gah->pa", wide, right_sum, precision=exact)
    small = jnp.concatenate(
        [left_weight.reshape(-1, LANES), right_weight.reshape(-1, LANES), bias_local]
    )
    small = sum_digit(small, "row", 1, 2)
    small = sum_digit(small, "row", 2, 2)
    small = sum_digit(small, "row", 4, 4)
    small = sum_digit(small, "col", 4, 4)
    small = sum_digit(small, "col", 1, 4)
    half = left_weight.size // LANES
    inverse = 1.0 / (owned * n_row * n_col)
    return (
        pair_delta,
        alignment_gradient,
        small[:half].reshape(left_weight.shape) * inverse,
        small[half : 2 * half].reshape(right_weight.shape) * inverse,
        total * inverse,
        small[2 * half] * inverse,
    )


def solution(mesh):
    placed = (P(("row", "col"), None, None), P(), P(), P(), P(), P("row", "col", None))
    return jax.shard_map(
        shards,
        mesh=mesh,
        in_specs=placed,
        out_specs=(P("row", "col", None), P(("row", "col"), None, None), P(), P(), P(), P()),
        check_vma=False,
    )
```

```python
import functools

import jax
import jax.numpy as jnp
from jax import lax
from jax.experimental import pallas as pl
from jax.experimental.pallas import tpu as pltpu
from jax.sharding import PartitionSpec as P

BF = jnp.bfloat16
F32 = jnp.float32
LANES = 128
VMEM = 56 * 1024 * 1024


def shift(x, axis, stride, size, k):
    n = lax.axis_size(axis)
    perm = []
    for i in range(n):
        digit = (i // stride) % size
        perm.append((i, i + stride * ((digit + k) % size - digit)))
    return lax.ppermute(x, axis, perm)


def digit_of(axis, stride, size):
    return lax.rem(lax.axis_index(axis) // stride, size)


def gather_digit(x, axis, stride, size):
    me = digit_of(axis, stride, size)
    parts = [x] + [shift(x, axis, stride, size, k) for k in range(1, size)]
    back = parts[::-1]
    ring = jnp.stack(back + back[:-1])
    return lax.dynamic_slice_in_dim(ring, size - 1 - me, size, 0)


def scatter_digit(x, axis, stride, size, link):
    me = digit_of(axis, stride, size)
    total = lax.dynamic_index_in_dim(x, me, 0, keepdims=False)
    for k in range(1, size):
        block = lax.dynamic_index_in_dim(x, lax.rem(me + k, size), 0, keepdims=False)
        total = total + shift(block.astype(link), axis, stride, size, k).astype(F32)
    return total


def swap_axes(x):
    n = lax.axis_size("row")
    return lax.ppermute(
        x, ("row", "col"), [(r * n + c, c * n + r) for r in range(n) for c in range(n)]
    )


def project(source, weight):
    return jnp.einsum("ket,ei->kit", source, weight, preferred_element_type=F32).astype(BF)


def padded_rows(t, rows):
    return jnp.concatenate([t, jnp.zeros((rows - t.shape[0], t.shape[1]), t.dtype)], axis=0)


def outer_grad_kernel(width, group, t_ref, w_ref, g_ref, bias_ref):
    @pl.when(pl.program_id(0) == 0)
    def _():
        bias_ref[...] = jnp.zeros_like(bias_ref)

    channels = w_ref.shape[0]
    total = jnp.zeros((1, LANES), F32)
    for pair in range(group // 2):
        a, b = t_ref[2 * pair], t_ref[2 * pair + 1]
        total = total + jnp.sum(a.astype(F32) + b.astype(F32), axis=0, keepdims=True)
        both = jnp.concatenate([padded_rows(a, LANES), padded_rows(b, LANES)], axis=0)
        grad = lax.dot_general(
            w_ref[...], both, (((1,), (1,)), ((), ())), preferred_element_type=F32
        ).astype(BF)
        for half in range(2):
            row = (2 * pair + half) * width
            for d in range(channels // width):
                g_ref[pl.ds(row, width), pl.ds(d * LANES, LANES)] = grad[
                    d * width : (d + 1) * width, half * LANES : (half + 1) * LANES
                ]
    bias_ref[...] += jnp.broadcast_to(total, bias_ref.shape)


def factor_grad_kernel(width, scale, steps, l_ref, r_ref, g_ref, gl_ref, gr_ref, acc_ref):
    step = pl.program_id(0)

    @pl.when(step == 0)
    def _():
        acc_ref[...] = jnp.zeros_like(acc_ref)

    grad = g_ref[...]
    gl_ref[...] = (jnp.dot(grad, r_ref[...], preferred_element_type=F32) * scale).astype(
        gl_ref.dtype
    )
    lt = l_ref[...].T
    chunk = 512
    for n in range(acc_ref.shape[1] // chunk):
        part = pl.ds(n * chunk, chunk)
        acc_ref[:, part] += jnp.dot(lt, g_ref[:, part], preferred_element_type=F32)

    @pl.when(step == steps - 1)
    def _():
        columns = gr_ref.shape[1]
        for d in range(gr_ref.shape[0]):
            block = acc_ref[:, d * LANES : (d + 1) * LANES].T
            gr_ref[d] = block[:columns].astype(gr_ref.dtype)


def pair_kernel(
    width, group, fresh, l_ref, r_ref, t_ref, wt_ref, off_ref, before_ref, sum_ref, p_ref, gw_ref,
    rt_ref, outer_ref,
):
    columns = t_ref.shape[1]
    depth = r_ref.shape[0] // LANES

    @pl.when(pl.program_id(0) == 0)
    def _():
        gw_ref[...] = jnp.zeros_like(gw_ref) if fresh else sum_ref[...]
        for d in range(depth):
            part = pl.ds(d * LANES, LANES)
            rt_ref[:, part] = r_ref[part, :].T

    per = 4
    for n in range(depth // per):
        block = jnp.dot(
            l_ref[...], rt_ref[:, pl.ds(n * per * LANES, per * LANES)], preferred_element_type=F32
        ).astype(BF)
        for i in range(group):
            for d in range(per):
                outer_ref[
                    i // 2,
                    pl.ds((n * per + d) * width, width),
                    pl.ds((i % 2) * LANES, LANES),
                ] = block[i * width : (i + 1) * width, d * LANES : (d + 1) * LANES]
    offset = off_ref[...]
    for pair in range(group // 2):
        outer = outer_ref[pair]
        out = jnp.dot(wt_ref[...], outer, preferred_element_type=F32).T
        p_ref[2 * pair] = (out[:columns] + offset).astype(BF)
        p_ref[2 * pair + 1] = (out[LANES : LANES + columns] + offset).astype(BF)
        both = jnp.concatenate(
            [padded_rows(t_ref[2 * pair], LANES), padded_rows(t_ref[2 * pair + 1], LANES)], axis=0
        )
        gw_ref[...] += jnp.dot(outer, both, preferred_element_type=F32)


def params():
    return pltpu.CompilerParams(
        dimension_semantics=("arbitrary",), vmem_limit_bytes=VMEM
    )


def outer_grads(cotangent, weight, width, first, count, before):
    rows, columns, out = cotangent.shape
    group = 8
    channels = weight.shape[0]
    depth = channels // width
    start = first // group
    in_specs = [
        pl.BlockSpec((group, columns, out), lambda i: (i + start, 0, 0)),
        pl.BlockSpec((channels, out), lambda i: (0, 0)),
    ]
    operands = [cotangent, weight]
    body = functools.partial(outer_grad_kernel, width, group)
    kernel = body
    if before is not None:
        in_specs.append(pl.BlockSpec(memory_space=pl.ANY))
        operands.append(before)

        def kernel(t_ref, w_ref, before_ref, *rest):
            body(t_ref, w_ref, *rest)

    return pl.pallas_call(
        kernel,
        grid=(count // group,),
        in_specs=in_specs,
        out_specs=[
            pl.BlockSpec((group * width, depth * LANES), lambda i: (i + start, 0)),
            pl.BlockSpec((8, out), lambda i: (0, 0)),
        ],
        out_shape=[
            jax.ShapeDtypeStruct((rows * width, depth * LANES), BF),
            jax.ShapeDtypeStruct((8, out), F32),
        ],
        input_output_aliases={} if before is None else {2: 0},
        compiler_params=params(),
        cost_estimate=pl.CostEstimate(
            flops=4 * count * columns * channels * out,
            bytes_accessed=(22 << 20) * count // rows,
            transcendentals=0,
        ),
        name="outer_grads",
    )(*operands)


def factor_grads(left, right, grad, width, columns, scale):
    rows, sequences = left.shape
    depth = right.shape[0] // LANES
    block = 512
    steps = rows // block
    return pl.pallas_call(
        functools.partial(factor_grad_kernel, width, scale, steps),
        grid=(steps,),
        in_specs=[
            pl.BlockSpec((block, sequences), lambda i: (i, 0)),
            pl.BlockSpec(right.shape, lambda i: (0, 0)),
            pl.BlockSpec((block, depth * LANES), lambda i: (i, 0)),
        ],
        out_specs=[
            pl.BlockSpec((block, sequences), lambda i: (i, 0)),
            pl.BlockSpec((depth, columns, sequences), lambda i: (0, 0, 0)),
        ],
        out_shape=[
            jax.ShapeDtypeStruct((rows, sequences), F32),
            jax.ShapeDtypeStruct((depth, columns, sequences), F32),
        ],
        scratch_shapes=[pltpu.VMEM((sequences, depth * LANES), F32)],
        compiler_params=params(),
        cost_estimate=pl.CostEstimate(
            flops=8 * rows * depth * LANES * sequences, bytes_accessed=24 << 20, transcendentals=0
        ),
        name="factor_grads",
    )(left, right, grad)


def pairs(left, right, cotangent, weight_t, offset, width, first, count, before):
    rows, columns, out = cotangent.shape
    sequences = left.shape[1]
    channels = weight_t.shape[1]
    group = 8
    depth = right.shape[0] // LANES
    start = first // group
    fresh = before is None
    in_specs = [
        pl.BlockSpec((group * width, sequences), lambda i: (i + start, 0)),
        pl.BlockSpec(right.shape, lambda i: (0, 0)),
        pl.BlockSpec((group, columns, out), lambda i: (i + start, 0, 0)),
        pl.BlockSpec((out, channels), lambda i: (0, 0)),
        pl.BlockSpec((1, out), lambda i: (0, 0)),
    ]
    operands = [left, right, cotangent, weight_t, offset]
    if fresh:

        def kernel(l_ref, r_ref, t_ref, wt_ref, off_ref, *rest):
            pair_kernel(
                width, group, fresh, l_ref, r_ref, t_ref, wt_ref, off_ref, None, None, *rest
            )
    else:
        kernel = functools.partial(pair_kernel, width, group, fresh)
        in_specs += [
            pl.BlockSpec(memory_space=pl.ANY),
            pl.BlockSpec((channels, out), lambda i: (0, 0)),
        ]
        operands += before
    return pl.pallas_call(
        kernel,
        grid=(count // group,),
        in_specs=in_specs,
        out_specs=[
            pl.BlockSpec((group, columns, out), lambda i: (i + start, 0, 0)),
            pl.BlockSpec((channels, out), lambda i: (0, 0)),
        ],
        out_shape=[
            jax.ShapeDtypeStruct((rows, columns, out), BF),
            jax.ShapeDtypeStruct((channels, out), F32),
        ],
        input_output_aliases={} if fresh else {5: 0},
        scratch_shapes=[
            pltpu.VMEM((sequences, depth * LANES), BF),
            pltpu.VMEM((group // 2, channels, 2 * LANES), BF),
        ],
        compiler_params=params(),
        cost_estimate=pl.CostEstimate(
            flops=12 * count * LANES * channels * out, bytes_accessed=3 << 20, transcendentals=0
        ),
        name="pairs",
    )(*operands)


def after(value, *others):
    return lax.optimization_barrier((value, *others))[0]


def shards(
    sequence_features,
    first_projection,
    second_projection,
    final_projection,
    final_offset,
    edge_change_cotangent,
):
    n_row = lax.axis_size("row")
    n_col = lax.axis_size("col")
    owned, _, sequences = sequence_features.shape
    rows, columns, out = edge_change_cotangent.shape
    width = first_projection.shape[1]
    scale = 1.0 / sequences

    weight = final_projection.reshape(width, width, out).swapaxes(0, 1).reshape(-1, out)
    weight_t = weight.T
    channels = weight.shape[0]
    offset = final_offset.reshape(1, out)

    swapped = swap_axes(sequence_features)
    left = project(sequence_features, first_projection) * jnp.asarray(scale, BF)
    half = rows // 2
    grad, bias_a = outer_grads(
        edge_change_cotangent, after(weight, left), width, 0, half, None
    )

    left = gather_digit(left, "col", 1, 4)
    right = project(swapped, second_projection)
    grad, bias_b = outer_grads(
        edge_change_cotangent, after(weight, left, right, bias_a), width, half, half, grad
    )

    left = gather_digit(left, "col", 4, 4)
    left = left.reshape(rows * width, sequences)
    right = gather_digit(right, "row", 4, 4)
    right = gather_digit(right, "row", 2, 2)
    right = gather_digit(right, "row", 1, 2)
    right = right.transpose(4, 2, 1, 0, 3, 5).reshape(width, columns, sequences)
    right = jnp.pad(right, ((0, 0), (0, LANES - columns), (0, 0))).reshape(-1, sequences)

    left_part, right_part = factor_grads(left, right, grad, width, columns, scale)

    left_sum = left_part.reshape(4, 4, owned, width, sequences)
    right_sum = right_part.reshape(width, 4, 2, 2, owned, sequences).transpose(3, 1, 2, 4, 0, 5)
    done = pairs(
        left, right, edge_change_cotangent, weight_t, after(offset, left_sum, right_sum),
        width, 0, 32, None,
    )
    left_sum = scatter_digit(left_sum, "col", 4, 4, BF)
    right_sum = scatter_digit(right_sum, "row", 1, 2, BF)
    done = pairs(
        left, right, edge_change_cotangent, weight_t, after(offset, left_sum, right_sum),
        width, 32, 24, done,
    )
    left_sum = scatter_digit(left_sum, "col", 1, 4, BF)
    right_sum = scatter_digit(right_sum, "row", 4, 4, BF)
    pair_delta, weight_part = pairs(
        left, right, edge_change_cotangent, weight_t, after(offset, left_sum, right_sum),
        width, 56, 24, done,
    )
    right_sum = scatter_digit(right_sum, "row", 2, 2, BF)

    exact = lax.Precision.HIGHEST
    left_weight = jnp.einsum(
        "gph,gah->pa", sequence_features.astype(F32), left_sum, precision=exact
    )
    right_weight = jnp.einsum("gph,gah->pa", swapped.astype(F32), right_sum, precision=exact)
    right_sum = swap_axes(right_sum)
    alignment_gradient = jnp.einsum(
        "awr,iw->air", left_sum, first_projection.astype(F32), precision=exact
    ) + jnp.einsum("awr,iw->air", right_sum, second_projection.astype(F32), precision=exact)

    small = jnp.concatenate(
        [left_weight.reshape(-1, LANES), right_weight.reshape(-1, LANES), bias_a + bias_b]
    )
    extra = small.shape[0]
    each = -(-extra // n_row)
    small = jnp.pad(small, ((0, each * n_row - extra), (0, 0))).reshape(n_row, each, LANES)
    main = channels // n_row
    pack = -(-(main + each) // 16) * 16
    total = jnp.concatenate([weight_part.reshape(n_row, main, out), small], axis=1)
    total = jnp.pad(total, ((0, 0), (0, pack - main - each), (0, 0))).astype(BF)
    for axis, share in (("row", False), ("col", True), ("row", True)):
        if share:
            total = jnp.broadcast_to(total[None], (n_row, pack, out))
        total = lax.all_to_all(total, axis, 0, 0, tiled=True)
        if axis == "col" or not share:
            total = jnp.sum(total.astype(F32), axis=0).astype(BF)
    total = total.astype(F32) * (1.0 / (owned * n_row * n_col))
    small = total[:, main : main + each].reshape(-1, LANES)
    total = total[:, :main].reshape(width, width, out).swapaxes(0, 1).reshape(channels, out)
    size = left_weight.size // LANES
    return (
        pair_delta,
        alignment_gradient,
        small[:size].reshape(left_weight.shape),
        small[size : 2 * size].reshape(right_weight.shape),
        total,
        small[2 * size],
    )


def solution(mesh):
    placed = (P(("row", "col"), None, None), P(), P(), P(), P(), P("row", "col", None))
    return jax.shard_map(
        shards,
        mesh=mesh,
        in_specs=placed,
        out_specs=(P("row", "col", None), P(("row", "col"), None, None), P(), P(), P(), P()),
        check_vma=False,
    )
```

```python
import functools

import jax
import jax.numpy as jnp
from jax import lax
from jax.experimental import pallas as pl
from jax.experimental.pallas import tpu as pltpu
from jax.sharding import PartitionSpec as P

BF = jnp.bfloat16
F32 = jnp.float32
LANES = 128
VMEM = 56 * 1024 * 1024


def exchange(x, axis):
    return lax.all_to_all(x, axis, 0, 0, tiled=True)


def gather_blocks(x, axis):
    return exchange(jnp.broadcast_to(x[None], (lax.axis_size(axis), *x.shape)), axis)


def scatter_blocks(x, axis):
    n = lax.axis_size(axis)
    x = exchange(x.reshape(n, x.shape[0] // n, *x.shape[1:]), axis)
    return jnp.sum(x.astype(F32), axis=0)


def swap_axes(x):
    n = lax.axis_size("row")
    return lax.ppermute(
        x, ("row", "col"), [(r * n + c, c * n + r) for r in range(n) for c in range(n)]
    )


def project_kernel(scale, x_ref, w_ref, out_ref):
    for n in range(x_ref.shape[0]):
        block = lax.dot_general(
            w_ref[...], x_ref[n], (((0,), (0,)), ((), ())), preferred_element_type=F32
        ).astype(BF)
        block = (block.astype(F32) * scale).astype(BF)
        for copy in range(out_ref.shape[0]):
            out_ref[copy, n] = block


def project_copies(source, weight, scale, copies):
    owned, _, sequences = source.shape
    return pl.pallas_call(
        functools.partial(project_kernel, scale),
        out_shape=jax.ShapeDtypeStruct((copies, owned, weight.shape[1], sequences), BF),
        compiler_params=pltpu.CompilerParams(vmem_limit_bytes=16 << 20),
        cost_estimate=pl.CostEstimate(flops=1 << 22, bytes_accessed=1 << 20, transcendentals=0),
        name="project_copies",
    )(source, weight)


def padded_rows(t, rows):
    return jnp.concatenate([t, jnp.zeros((rows - t.shape[0], t.shape[1]), t.dtype)], axis=0)


def outer_grad_kernel(width, group, t_ref, w_ref, g_ref, bias_ref):
    @pl.when(pl.program_id(0) == 0)
    def _():
        bias_ref[...] = jnp.zeros_like(bias_ref)

    channels = w_ref.shape[0]
    total = jnp.zeros((1, LANES), F32)
    for pair in range(group // 2):
        a, b = t_ref[2 * pair], t_ref[2 * pair + 1]
        total = total + jnp.sum(a.astype(F32) + b.astype(F32), axis=0, keepdims=True)
        both = jnp.concatenate([padded_rows(a, LANES), padded_rows(b, LANES)], axis=0)
        grad = lax.dot_general(
            w_ref[...], both, (((1,), (1,)), ((), ())), preferred_element_type=F32
        ).astype(BF)
        for half in range(2):
            row = (2 * pair + half) * width
            for d in range(channels // width):
                g_ref[pl.ds(row, width), pl.ds(d * LANES, LANES)] = grad[
                    d * width : (d + 1) * width, half * LANES : (half + 1) * LANES
                ]
    bias_ref[...] += jnp.broadcast_to(total, bias_ref.shape)


def stream(hbm_ref, buf_ref, sem_ref, pieces):
    rows = buf_ref.shape[0] // pieces
    out = []
    for k in range(pieces):
        part = pl.ds(k * rows, rows)
        copy = pltpu.make_async_copy(hbm_ref.at[part], buf_ref.at[part], sem_ref.at[k])
        copy.start()
        out.append((part, copy))
    return out


def left_grad_kernel(scale, pieces, r_ref, g_ref, out_ref, buf_ref, pad_ref, sem_ref):
    copies = stream(g_ref, buf_ref, sem_ref, pieces)
    columns, sequences = r_ref.shape[1:]
    for d in range(r_ref.shape[0]):
        pad_ref[pl.ds(d * LANES, LANES)] = padded_rows(r_ref[d], LANES)
    for part, copy in copies:
        copy.wait()
        out_ref[part] = (
            jnp.dot(buf_ref[part], pad_ref[...], preferred_element_type=F32) * scale
        ).astype(out_ref.dtype)


def right_grad_kernel(pieces, l_ref, g_ref, out_ref, buf_ref, acc_ref, sem_ref):
    copies = stream(g_ref, buf_ref, sem_ref, pieces)
    chunk = 512
    for k, (part, copy) in enumerate(copies):
        lt = l_ref[part].T
        copy.wait()
        for n in range(acc_ref.shape[1] // chunk):
            lanes = pl.ds(n * chunk, chunk)
            term = jnp.dot(lt, buf_ref[part, lanes], preferred_element_type=F32)
            acc_ref[:, lanes] = term if k == 0 else acc_ref[:, lanes] + term
    columns = out_ref.shape[1]
    for d in range(out_ref.shape[0]):
        block = acc_ref[:, d * LANES : (d + 1) * LANES].T
        out_ref[d] = block[:columns].astype(out_ref.dtype)


def pair_kernel(
    width, group, l_ref, r_ref, t_ref, wt_ref, off_ref, p_ref, gw_ref, rt_ref, outer_ref
):
    columns = t_ref.shape[1]
    depth = r_ref.shape[0]

    @pl.when(pl.program_id(0) == 0)
    def _():
        gw_ref[...] = jnp.zeros_like(gw_ref)
        for d in range(depth):
            rt_ref[:, pl.ds(d * LANES, LANES)] = padded_rows(r_ref[d], LANES).T

    per = 4
    for n in range(depth // per):
        block = jnp.dot(
            l_ref[...], rt_ref[:, pl.ds(n * per * LANES, per * LANES)], preferred_element_type=F32
        ).astype(BF)
        for i in range(group):
            for d in range(per):
                outer_ref[pl.ds((n * per + d) * width, width), pl.ds(i * LANES, LANES)] = block[
                    i * width : (i + 1) * width, d * LANES : (d + 1) * LANES
                ]
    offset = off_ref[...]
    out = jnp.dot(wt_ref[...], outer_ref[...], preferred_element_type=F32)
    for i in range(group):
        p_ref[i] = (out[:, i * LANES : (i + 1) * LANES].T[:columns] + offset).astype(BF)
    cotangent = jnp.concatenate([padded_rows(t_ref[i], LANES) for i in range(group)], axis=0)
    step = 256
    for n in range(gw_ref.shape[0] // step):
        part = pl.ds(n * step, step)
        gw_ref[part] += jnp.dot(outer_ref[part], cotangent, preferred_element_type=F32)


def params():
    return pltpu.CompilerParams(
        dimension_semantics=("arbitrary",), vmem_limit_bytes=VMEM
    )


def outer_grads(cotangent, weight, width):
    rows, columns, out = cotangent.shape
    group = 16
    channels = weight.shape[0]
    depth = channels // width
    return pl.pallas_call(
        functools.partial(outer_grad_kernel, width, group),
        grid=(rows // group,),
        in_specs=[
            pl.BlockSpec((group, columns, out), lambda i: (i, 0, 0)),
            pl.BlockSpec((channels, out), lambda i: (0, 0)),
        ],
        out_specs=[
            pl.BlockSpec((group * width, depth * LANES), lambda i: (i, 0)),
            pl.BlockSpec((8, out), lambda i: (0, 0)),
        ],
        out_shape=[
            jax.ShapeDtypeStruct((rows * width, depth * LANES), BF),
            jax.ShapeDtypeStruct((8, out), F32),
        ],
        compiler_params=params(),
        cost_estimate=pl.CostEstimate(
            flops=4 * rows * columns * channels * out, bytes_accessed=22 << 20, transcendentals=0
        ),
        name="outer_grads",
    )(cotangent, weight)


def left_grads(right, grad, scale):
    rows, depth = grad.shape
    sequences = right.shape[2]
    pieces = 10
    return pl.pallas_call(
        functools.partial(left_grad_kernel, scale, pieces),
        in_specs=[
            pl.BlockSpec(memory_space=pltpu.VMEM),
            pl.BlockSpec(memory_space=pl.ANY),
        ],
        out_specs=pl.BlockSpec(memory_space=pltpu.VMEM),
        out_shape=jax.ShapeDtypeStruct((rows, sequences), BF),
        scratch_shapes=[
            pltpu.VMEM((rows, depth), BF),
            pltpu.VMEM((depth, sequences), BF),
            pltpu.SemaphoreType.DMA((pieces,)),
        ],
        compiler_params=pltpu.CompilerParams(vmem_limit_bytes=VMEM),
        cost_estimate=pl.CostEstimate(
            flops=4 * rows * depth * sequences, bytes_accessed=22 << 20, transcendentals=0
        ),
        name="left_grads",
    )(right, grad)


def right_grads(left, grad, columns):
    rows, sequences = left.shape
    depth = grad.shape[1]
    pieces = 10
    return pl.pallas_call(
        functools.partial(right_grad_kernel, pieces),
        in_specs=[
            pl.BlockSpec(memory_space=pltpu.VMEM),
            pl.BlockSpec(memory_space=pl.ANY),
        ],
        out_specs=pl.BlockSpec(memory_space=pltpu.VMEM),
        out_shape=jax.ShapeDtypeStruct((depth // LANES, columns, sequences), BF),
        scratch_shapes=[
            pltpu.VMEM((rows, depth), BF),
            pltpu.VMEM((sequences, depth), F32),
            pltpu.SemaphoreType.DMA((pieces,)),
        ],
        compiler_params=pltpu.CompilerParams(vmem_limit_bytes=VMEM),
        cost_estimate=pl.CostEstimate(
            flops=4 * rows * depth * sequences, bytes_accessed=22 << 20, transcendentals=0
        ),
        name="right_grads",
    )(left, grad)


def pairs(left, right, cotangent, weight_t, offset, width):
    rows, columns, out = cotangent.shape
    sequences = left.shape[1]
    channels = weight_t.shape[1]
    group = 20
    depth = right.shape[0]
    return pl.pallas_call(
        functools.partial(pair_kernel, width, group),
        grid=(rows // group,),
        in_specs=[
            pl.BlockSpec((group * width, sequences), lambda i: (i, 0)),
            pl.BlockSpec(right.shape, lambda i: (0, 0, 0)),
            pl.BlockSpec((group, columns, out), lambda i: (i, 0, 0)),
            pl.BlockSpec((out, channels), lambda i: (0, 0)),
            pl.BlockSpec((1, out), lambda i: (0, 0)),
        ],
        out_specs=[
            pl.BlockSpec((group, columns, out), lambda i: (i, 0, 0)),
            pl.BlockSpec((channels, out), lambda i: (0, 0)),
        ],
        out_shape=[
            jax.ShapeDtypeStruct((rows, columns, out), BF),
            jax.ShapeDtypeStruct((channels, out), F32),
        ],
        scratch_shapes=[
            pltpu.VMEM((sequences, depth * LANES), BF),
            pltpu.VMEM((channels, group * LANES), BF),
        ],
        compiler_params=params(),
        cost_estimate=pl.CostEstimate(
            flops=12 * rows * LANES * channels * out, bytes_accessed=6 << 20, transcendentals=0
        ),
        name="pairs",
    )(left, right, cotangent, weight_t, offset)


def after(value, *others):
    return lax.optimization_barrier((value, *others))[0]


def shards(
    sequence_features,
    first_projection,
    second_projection,
    final_projection,
    final_offset,
    edge_change_cotangent,
):
    n_row = lax.axis_size("row")
    n_col = lax.axis_size("col")
    owned, _, sequences = sequence_features.shape
    rows, columns, out = edge_change_cotangent.shape
    width = first_projection.shape[1]
    scale = 1.0 / sequences

    weight = final_projection.reshape(width, width, out).swapaxes(0, 1).reshape(-1, out)
    weight_t = weight.T
    channels = weight.shape[0]
    offset = final_offset.reshape(1, out)

    swapped = swap_axes(sequence_features)
    left = project_copies(sequence_features, first_projection, scale, n_col)
    grad, bias_local = outer_grads(edge_change_cotangent, after(weight, left), width)
    left = exchange(left, "col").reshape(rows * width, sequences)

    right = project_copies(
        swapped, after(second_projection, bias_local, weight_t), 1.0, n_row
    )
    right = exchange(right, "row").reshape(columns, width, sequences).swapaxes(0, 1)

    right_part = right_grads(left, grad, columns)
    left_part = left_grads(after(right, right_part), grad, scale)
    right_sum = scatter_blocks(right_part.swapaxes(0, 1), "row")

    pair_delta, weight_part = pairs(
        left, right, edge_change_cotangent, weight_t, after(offset, left_part, right_sum), width
    )
    left_sum = scatter_blocks(left_part.reshape(rows, width, sequences), "col")

    exact = lax.Precision.HIGHEST
    left_weight = jnp.einsum(
        "gph,gah->ap", sequence_features.astype(F32), left_sum, precision=exact
    )
    right_weight = jnp.einsum("gph,gah->ap", swapped.astype(F32), right_sum, precision=exact)
    right_sum = swap_axes(right_sum)
    alignment_gradient = jnp.einsum(
        "awr,iw->air", left_sum, first_projection.astype(F32), precision=exact
    ) + jnp.einsum("awr,iw->air", right_sum, second_projection.astype(F32), precision=exact)

    small = jnp.concatenate(
        [left_weight.reshape(-1, LANES), right_weight.reshape(-1, LANES), bias_local]
    )
    extra = small.shape[0]
    each = -(-extra // n_row)
    small = jnp.pad(small, ((0, each * n_row - extra), (0, 0))).reshape(n_row, each, LANES)
    main = channels // n_row
    pack = -(-(main + each) // 8) * 8
    total = jnp.concatenate([weight_part.reshape(n_row, main, out), small], axis=1)
    total = jnp.pad(total, ((0, 0), (0, pack - main - each), (0, 0))).astype(BF)
    total = scatter_blocks(total.reshape(n_row * pack, out), "row").astype(BF)
    total = jnp.sum(gather_blocks(total, "col").astype(F32), axis=0).astype(BF)
    total = gather_blocks(total, "row")
    total = total.astype(F32) * (1.0 / (owned * n_row * n_col))
    small = total[:, main : main + each].reshape(-1, LANES)
    total = total[:, :main].reshape(width, width, out).swapaxes(0, 1).reshape(channels, out)
    size = left_weight.size // LANES
    return (
        pair_delta,
        alignment_gradient,
        small[:size].reshape(left_weight.shape).T,
        small[size : 2 * size].reshape(right_weight.shape).T,
        total,
        small[2 * size],
    )


def solution(mesh):
    placed = (P(("row", "col"), None, None), P(), P(), P(), P(), P("row", "col", None))
    return jax.shard_map(
        shards,
        mesh=mesh,
        in_specs=placed,
        out_specs=(P("row", "col", None), P(("row", "col"), None, None), P(), P(), P(), P()),
        check_vma=False,
    )
```

```python
import functools

import jax
import jax.numpy as jnp
from jax import lax
from jax.experimental import pallas as pl
from jax.experimental.pallas import tpu as pltpu
from jax.sharding import PartitionSpec as P

BF = jnp.bfloat16
F32 = jnp.float32
LANES = 128
VMEM = 56 * 1024 * 1024


def exchange(x, axis):
    return lax.all_to_all(x, axis, 0, 0, tiled=True)


def gather_blocks(x, axis):
    return exchange(jnp.broadcast_to(x[None], (lax.axis_size(axis), *x.shape)), axis)


def scatter_blocks(x, axis):
    n = lax.axis_size(axis)
    x = exchange(x.reshape(n, x.shape[0] // n, *x.shape[1:]), axis)
    return jnp.sum(x.astype(F32), axis=0)


def swap_axes(x):
    n = lax.axis_size("row")
    return lax.ppermute(
        x, ("row", "col"), [(r * n + c, c * n + r) for r in range(n) for c in range(n)]
    )


def project_kernel(scale, x_ref, first_ref, second_ref, left_ref, right_ref):
    for n in range(x_ref.shape[0]):
        x = x_ref[n]
        left = jnp.dot(first_ref[...], x, preferred_element_type=F32).astype(BF)
        left = (left.astype(F32) * scale).astype(BF)
        for copy in range(left_ref.shape[0]):
            left_ref[copy, n] = left
        right_ref[n] = jnp.dot(second_ref[...], x, preferred_element_type=F32).astype(BF)


def project(source, first, second, scale, copies):
    owned, _, sequences = source.shape
    width = first.shape[0]
    return pl.pallas_call(
        functools.partial(project_kernel, scale),
        out_shape=[
            jax.ShapeDtypeStruct((copies, owned, width, sequences), BF),
            jax.ShapeDtypeStruct((owned, width, sequences), BF),
        ],
        compiler_params=pltpu.CompilerParams(vmem_limit_bytes=16 << 20),
        cost_estimate=pl.CostEstimate(flops=1 << 22, bytes_accessed=1 << 20, transcendentals=0),
        name="project",
    )(source, first, second)


def unpack_kernel(inverse, pack_ref, weight_ref, left_ref, right_ref, bias_ref):
    width = weight_ref.shape[0]
    blocks = pack_ref.shape[0]
    main = weight_ref.shape[0] * weight_ref.shape[1] // blocks
    each = width // blocks
    total = [pack_ref[n].astype(F32) * inverse for n in range(blocks)]
    weight = jnp.concatenate([t[:main] for t in total], axis=0).reshape(weight_ref.shape)
    weight_ref[...] = jnp.swapaxes(weight, 0, 1)
    half = left_ref.shape[1]
    for n in range(blocks):
        rows = total[n][main : main + each]
        left_ref[pl.ds(n * each, each)] = rows[:, :half]
        right_ref[pl.ds(n * each, each)] = rows[:, half:]
    bias_ref[...] = total[0][main + each : main + each + 1]


def unpack(packed, width, half, inverse):
    out = packed.shape[2]
    return pl.pallas_call(
        functools.partial(unpack_kernel, inverse),
        out_shape=[
            jax.ShapeDtypeStruct((width, width, out), F32),
            jax.ShapeDtypeStruct((width, half), F32),
            jax.ShapeDtypeStruct((width, half), F32),
            jax.ShapeDtypeStruct((1, out), F32),
        ],
        compiler_params=pltpu.CompilerParams(vmem_limit_bytes=16 << 20),
        cost_estimate=pl.CostEstimate(flops=1 << 20, bytes_accessed=1 << 20, transcendentals=0),
        name="unpack",
    )(packed)


def padded_rows(t, rows):
    return jnp.concatenate([t, jnp.zeros((rows - t.shape[0], t.shape[1]), t.dtype)], axis=0)


def outer_grad_kernel(width, pieces, t_ref, w_ref, g_ref, bias_ref, buf_ref, sem_ref):
    channels = w_ref.shape[0]
    group = t_ref.shape[0] // pieces
    total = jnp.zeros((1, LANES), F32)
    copies = []
    for k in range(pieces):
        for first in range(k * group, (k + 1) * group, 2):
            a, b = t_ref[first], t_ref[first + 1]
            total = total + jnp.sum(a.astype(F32) + b.astype(F32), axis=0, keepdims=True)
            both = jnp.concatenate([padded_rows(a, LANES), padded_rows(b, LANES)], axis=0)
            grad = lax.dot_general(
                w_ref[...], both, (((1,), (1,)), ((), ())), preferred_element_type=F32
            ).astype(BF)
            for half in range(2):
                row = (first + half) * width
                for d in range(channels // width):
                    buf_ref[pl.ds(row, width), pl.ds(d * LANES, LANES)] = grad[
                        d * width : (d + 1) * width, half * LANES : (half + 1) * LANES
                    ]
        part = pl.ds(k * group * width, group * width)
        copy = pltpu.make_async_copy(buf_ref.at[part], g_ref.at[part], sem_ref.at[k])
        copy.start()
        copies.append(copy)
    bias_ref[...] = jnp.broadcast_to(total, bias_ref.shape)
    for copy in copies:
        copy.wait()


def stream(hbm_ref, buf_ref, sem_ref, pieces):
    rows = buf_ref.shape[0] // pieces
    out = []
    for k in range(pieces):
        part = pl.ds(k * rows, rows)
        copy = pltpu.make_async_copy(hbm_ref.at[part], buf_ref.at[part], sem_ref.at[k])
        copy.start()
        out.append((part, copy))
    return out


def left_grad_kernel(scale, pieces, r_ref, g_ref, out_ref, panel_ref, buf_ref, pad_ref, sem_ref):
    copies = stream(g_ref, buf_ref, sem_ref, pieces)
    panel = jnp.swapaxes(r_ref[...].astype(F32), 0, 1).astype(BF)
    panel_ref[...] = panel
    for d in range(panel.shape[0]):
        pad_ref[pl.ds(d * LANES, LANES)] = padded_rows(panel[d], LANES)
    for part, copy in copies:
        copy.wait()
        out_ref[part] = (
            jnp.dot(buf_ref[part], pad_ref[...], preferred_element_type=F32) * scale
        ).astype(out_ref.dtype)


def right_grad_kernel(pieces, l_ref, g_ref, out_ref, buf_ref, acc_ref, block_ref, sem_ref):
    copies = stream(g_ref, buf_ref, sem_ref, pieces)
    chunk = 512
    for k, (part, copy) in enumerate(copies):
        lt = l_ref[part].T
        copy.wait()
        for n in range(acc_ref.shape[1] // chunk):
            lanes = pl.ds(n * chunk, chunk)
            term = jnp.dot(lt, buf_ref[part, lanes], preferred_element_type=F32)
            acc_ref[:, lanes] = term if k == 0 else acc_ref[:, lanes] + term
    columns, depth = out_ref.shape[:2]
    group = 8
    for first in range(0, depth, group):
        blocks = [
            acc_ref[:, d * LANES : (d + 1) * LANES].T[:columns]
            for d in range(first, first + group)
        ]
        block_ref[:, pl.ds(first, group)] = jnp.swapaxes(jnp.stack(blocks), 0, 1)
    out_ref[...] = block_ref[...].astype(out_ref.dtype)


def pair_kernel(
    width, group, l_ref, r_ref, t_ref, w_ref, off_ref, p_ref, pack_ref, gw_ref, wt_ref, rt_ref,
    outer_ref,
):
    columns = t_ref.shape[1]
    depth = r_ref.shape[0]

    @pl.when(pl.program_id(0) == 0)
    def _():
        gw_ref[...] = jnp.zeros_like(gw_ref)
        for n in range(w_ref.shape[0] // LANES):
            part = pl.ds(n * LANES, LANES)
            wt_ref[:, part] = w_ref[part].T
        for d in range(depth):
            rt_ref[:, pl.ds(d * LANES, LANES)] = padded_rows(r_ref[d], LANES).T

    per = 4
    for n in range(depth // per):
        block = jnp.dot(
            l_ref[...], rt_ref[:, pl.ds(n * per * LANES, per * LANES)], preferred_element_type=F32
        ).astype(BF)
        for i in range(group):
            for d in range(per):
                outer_ref[pl.ds((n * per + d) * width, width), pl.ds(i * LANES, LANES)] = block[
                    i * width : (i + 1) * width, d * LANES : (d + 1) * LANES
                ]
    offset = off_ref[...]
    out = jnp.dot(wt_ref[...], outer_ref[...], preferred_element_type=F32)
    for i in range(group):
        p_ref[i] = (out[:, i * LANES : (i + 1) * LANES].T[:columns] + offset).astype(BF)
    cotangent = jnp.concatenate([padded_rows(t_ref[i], LANES) for i in range(group)], axis=0)
    step = 256
    for n in range(gw_ref.shape[0] // step):
        part = pl.ds(n * step, step)
        gw_ref[part] += jnp.dot(outer_ref[part], cotangent, preferred_element_type=F32)

    @pl.when(pl.program_id(0) == pl.num_programs(0) - 1)
    def _():
        blocks, pack, out = pack_ref.shape
        main = gw_ref.shape[0] // blocks
        for n in range(blocks):
            block = padded_rows(gw_ref[pl.ds(n * main, main)], pack)
            pack_ref[n] = block.astype(BF)


def params():
    return pltpu.CompilerParams(
        dimension_semantics=("arbitrary",), vmem_limit_bytes=VMEM
    )


def outer_grads(cotangent, weight, width):
    rows, columns, out = cotangent.shape
    pieces = 10
    channels = weight.shape[0]
    depth = channels // width
    return pl.pallas_call(
        functools.partial(outer_grad_kernel, width, pieces),
        in_specs=[pl.BlockSpec(memory_space=pltpu.VMEM)] * 2,
        out_specs=[
            pl.BlockSpec(memory_space=pl.ANY),
            pl.BlockSpec(memory_space=pltpu.VMEM),
        ],
        out_shape=[
            jax.ShapeDtypeStruct((rows * width, depth * LANES), BF),
            jax.ShapeDtypeStruct((8, out), F32),
        ],
        scratch_shapes=[
            pltpu.VMEM((rows * width, depth * LANES), BF),
            pltpu.SemaphoreType.DMA((pieces,)),
        ],
        compiler_params=pltpu.CompilerParams(vmem_limit_bytes=VMEM),
        cost_estimate=pl.CostEstimate(
            flops=4 * rows * columns * channels * out, bytes_accessed=22 << 20, transcendentals=0
        ),
        name="outer_grads",
    )(cotangent, weight)


def left_grads(right, grad, scale):
    rows, depth = grad.shape
    sequences = right.shape[2]
    pieces = 10
    return pl.pallas_call(
        functools.partial(left_grad_kernel, scale, pieces),
        in_specs=[
            pl.BlockSpec(memory_space=pltpu.VMEM),
            pl.BlockSpec(memory_space=pl.ANY),
        ],
        out_specs=[pl.BlockSpec(memory_space=pltpu.VMEM)] * 2,
        out_shape=[
            jax.ShapeDtypeStruct((rows, sequences), BF),
            jax.ShapeDtypeStruct((right.shape[1], right.shape[0], sequences), BF),
        ],
        scratch_shapes=[
            pltpu.VMEM((rows, depth), BF),
            pltpu.VMEM((depth, sequences), BF),
            pltpu.SemaphoreType.DMA((pieces,)),
        ],
        compiler_params=pltpu.CompilerParams(vmem_limit_bytes=VMEM),
        cost_estimate=pl.CostEstimate(
            flops=4 * rows * depth * sequences, bytes_accessed=22 << 20, transcendentals=0
        ),
        name="left_grads",
    )(right, grad)


def right_grads(left, grad, columns):
    rows, sequences = left.shape
    depth = grad.shape[1]
    pieces = 10
    return pl.pallas_call(
        functools.partial(right_grad_kernel, pieces),
        in_specs=[
            pl.BlockSpec(memory_space=pltpu.VMEM),
            pl.BlockSpec(memory_space=pl.ANY),
        ],
        out_specs=pl.BlockSpec(memory_space=pltpu.VMEM),
        out_shape=jax.ShapeDtypeStruct((columns, depth // LANES, sequences), BF),
        scratch_shapes=[
            pltpu.VMEM((rows, depth), BF),
            pltpu.VMEM((sequences, depth), F32),
            pltpu.VMEM((columns, depth // LANES, sequences), F32),
            pltpu.SemaphoreType.DMA((pieces,)),
        ],
        compiler_params=pltpu.CompilerParams(vmem_limit_bytes=VMEM),
        cost_estimate=pl.CostEstimate(
            flops=4 * rows * depth * sequences, bytes_accessed=22 << 20, transcendentals=0
        ),
        name="right_grads",
    )(left, grad)


def pairs(left, right, cotangent, weight, offset, width, blocks, pack):
    rows, columns, out = cotangent.shape
    sequences = left.shape[1]
    channels = weight.shape[0]
    group = 20
    depth = right.shape[0]
    return pl.pallas_call(
        functools.partial(pair_kernel, width, group),
        grid=(rows // group,),
        in_specs=[
            pl.BlockSpec((group * width, sequences), lambda i: (i, 0)),
            pl.BlockSpec(right.shape, lambda i: (0, 0, 0)),
            pl.BlockSpec((group, columns, out), lambda i: (i, 0, 0)),
            pl.BlockSpec((channels, out), lambda i: (0, 0)),
            pl.BlockSpec((1, out), lambda i: (0, 0)),
        ],
        out_specs=[
            pl.BlockSpec((group, columns, out), lambda i: (i, 0, 0)),
            pl.BlockSpec((blocks, pack, out), lambda i: (0, 0, 0)),
        ],
        out_shape=[
            jax.ShapeDtypeStruct((rows, columns, out), BF),
            jax.ShapeDtypeStruct((blocks, pack, out), BF),
        ],
        scratch_shapes=[
            pltpu.VMEM((channels, out), F32),
            pltpu.VMEM((out, channels), BF),
            pltpu.VMEM((sequences, depth * LANES), BF),
            pltpu.VMEM((channels, group * LANES), BF),
        ],
        compiler_params=params(),
        cost_estimate=pl.CostEstimate(
            flops=12 * rows * LANES * channels * out, bytes_accessed=6 << 20, transcendentals=0
        ),
        name="pairs",
    )(left, right, cotangent, weight, offset)


def after(value, *others):
    return lax.optimization_barrier((value, *others))[0]


def shards(
    sequence_features,
    first_projection,
    second_projection,
    final_projection,
    final_offset,
    edge_change_cotangent,
):
    n_row = lax.axis_size("row")
    n_col = lax.axis_size("col")
    owned, _, sequences = sequence_features.shape
    rows, columns, out = edge_change_cotangent.shape
    width = first_projection.shape[1]
    scale = 1.0 / sequences

    weight = final_projection.reshape(width, width, out).swapaxes(0, 1).reshape(-1, out)
    channels = weight.shape[0]
    offset = final_offset.reshape(1, out)

    left, right = project(
        sequence_features, first_projection.T, second_projection.T, scale, n_col
    )
    right = swap_axes(right)
    grad, bias_local = outer_grads(edge_change_cotangent, after(weight, left), width)
    left = exchange(left, "col").reshape(rows * width, sequences)

    right = gather_blocks(after(right, bias_local), "row").reshape(columns, width, sequences)

    right_part = right_grads(left, grad, columns)
    left_part, panel = left_grads(after(right, right_part), grad, scale)
    right_sum = scatter_blocks(right_part, "row")

    each = width // n_row
    main = channels // n_row
    pack = -(-(main + each + 1) // 8) * 8
    pair_delta, total = pairs(
        left, panel, edge_change_cotangent, weight, after(offset, left_part, right_sum), width,
        n_row, pack,
    )
    left_sum = scatter_blocks(left_part.reshape(rows, width, sequences), "col")

    exact = lax.Precision.HIGHEST
    left_weight = jnp.einsum(
        "gph,gah->ap", sequence_features.astype(F32), left_sum, precision=exact
    )
    right_back = swap_axes(right_sum)
    right_weight = jnp.einsum(
        "gph,gah->ap", sequence_features.astype(F32), right_back, precision=exact
    )

    small = jnp.concatenate([left_weight, right_weight], axis=1).reshape(n_row, each, LANES)
    bias = jnp.pad(bias_local[:1][None], ((0, n_row - 1), (0, 0), (0, 0)))
    small = jnp.concatenate([small, bias], axis=1).astype(BF)
    total = total + jnp.pad(small, ((0, 0), (main, pack - main - each - 1), (0, 0)))
    total = scatter_blocks(total.reshape(n_row * pack, out), "row").astype(BF)
    alignment_gradient = jnp.einsum(
        "awr,iw->air", left_sum, first_projection.astype(F32), precision=exact
    ) + jnp.einsum("awr,iw->air", right_back, second_projection.astype(F32), precision=exact)
    total = jnp.sum(gather_blocks(total, "col").astype(F32), axis=0).astype(BF)
    total = gather_blocks(total, "row")
    total, left_weight, right_weight, bias = unpack(
        total, width, left_weight.shape[1], 1.0 / (owned * n_row * n_col)
    )
    return (
        pair_delta,
        alignment_gradient,
        left_weight.T,
        right_weight.T,
        total.reshape(channels, out),
        bias.reshape(out),
    )


def solution(mesh):
    placed = (P(("row", "col"), None, None), P(), P(), P(), P(), P("row", "col", None))
    return jax.shard_map(
        shards,
        mesh=mesh,
        in_specs=placed,
        out_specs=(P("row", "col", None), P(("row", "col"), None, None), P(), P(), P(), P()),
        check_vma=False,
    )
```

```python
import functools

import jax
import jax.numpy as jnp
from jax import lax
from jax.experimental import pallas as pl
from jax.experimental.pallas import tpu as pltpu
from jax.sharding import PartitionSpec as P

BF = jnp.bfloat16
F32 = jnp.float32
LANES = 128
VMEM = 56 * 1024 * 1024


def exchange(x, axis):
    return lax.all_to_all(x, axis, 0, 0, tiled=True)


def gather_blocks(x, axis):
    return exchange(jnp.broadcast_to(x[None], (lax.axis_size(axis), *x.shape)), axis)


def scatter_blocks(x, axis):
    n = lax.axis_size(axis)
    x = exchange(x.reshape(n, x.shape[0] // n, *x.shape[1:]), axis)
    return jnp.sum(x.astype(F32), axis=0)


def swap_axes(x):
    n = lax.axis_size("row")
    return lax.ppermute(
        x, ("row", "col"), [(r * n + c, c * n + r) for r in range(n) for c in range(n)]
    )


def project_kernel(scale, x_ref, first_ref, second_ref, left_ref, right_ref):
    for n in range(x_ref.shape[0]):
        x = x_ref[n]
        left = jnp.dot(first_ref[...], x, preferred_element_type=F32).astype(BF)
        left = (left.astype(F32) * scale).astype(BF)
        for copy in range(left_ref.shape[0]):
            left_ref[copy, n] = left
        right_ref[n] = jnp.dot(second_ref[...], x, preferred_element_type=F32).astype(BF)


def project(source, first, second, scale, copies):
    owned, _, sequences = source.shape
    width = first.shape[0]
    return pl.pallas_call(
        functools.partial(project_kernel, scale),
        out_shape=[
            jax.ShapeDtypeStruct((copies, owned, width, sequences), BF),
            jax.ShapeDtypeStruct((owned, width, sequences), BF),
        ],
        compiler_params=pltpu.CompilerParams(vmem_limit_bytes=VMEM),
        cost_estimate=pl.CostEstimate(flops=1 << 22, bytes_accessed=1 << 20, transcendentals=0),
        name="project",
    )(source, first, second)


def unpack_kernel(inverse, pack_ref, weight_ref, left_ref, right_ref, bias_ref):
    width = weight_ref.shape[0]
    blocks = pack_ref.shape[0]
    main = weight_ref.shape[0] * weight_ref.shape[1] // blocks
    each = width // blocks
    total = [pack_ref[n].astype(F32) * inverse for n in range(blocks)]
    weight = jnp.concatenate([t[:main] for t in total], axis=0).reshape(weight_ref.shape)
    weight_ref[...] = jnp.swapaxes(weight, 0, 1)
    half = left_ref.shape[1]
    for n in range(blocks):
        rows = total[n][main : main + each]
        left_ref[pl.ds(n * each, each)] = rows[:, :half]
        right_ref[pl.ds(n * each, each)] = rows[:, half:]
    bias_ref[...] = total[0][main + each : main + each + 1]


def unpack(packed, width, half, inverse):
    out = packed.shape[2]
    return pl.pallas_call(
        functools.partial(unpack_kernel, inverse),
        out_shape=[
            jax.ShapeDtypeStruct((width, width, out), F32),
            jax.ShapeDtypeStruct((width, half), F32),
            jax.ShapeDtypeStruct((width, half), F32),
            jax.ShapeDtypeStruct((1, out), F32),
        ],
        compiler_params=pltpu.CompilerParams(vmem_limit_bytes=16 << 20),
        cost_estimate=pl.CostEstimate(flops=1 << 20, bytes_accessed=1 << 20, transcendentals=0),
        name="unpack",
    )(packed)


def padded_rows(t, rows):
    return jnp.concatenate([t, jnp.zeros((rows - t.shape[0], t.shape[1]), t.dtype)], axis=0)


def outer_grad_kernel(
    width, pieces, t_ref, natural_ref, g_ref, bias_ref, w_ref, buf_ref, sem_ref
):
    channels = w_ref.shape[0]
    swapped = jnp.swapaxes(natural_ref[...].astype(F32), 0, 1)
    w_ref[...] = swapped.reshape(w_ref.shape).astype(BF)
    group = t_ref.shape[0] // pieces
    total = jnp.zeros((1, LANES), F32)
    copies = []
    for k in range(pieces):
        for first in range(k * group, (k + 1) * group, 2):
            a, b = t_ref[first], t_ref[first + 1]
            total = total + jnp.sum(a.astype(F32) + b.astype(F32), axis=0, keepdims=True)
            both = jnp.concatenate([padded_rows(a, LANES), padded_rows(b, LANES)], axis=0)
            grad = lax.dot_general(
                w_ref[...], both, (((1,), (1,)), ((), ())), preferred_element_type=F32
            ).astype(BF)
            for half in range(2):
                row = (first + half) * width
                for d in range(channels // width):
                    buf_ref[pl.ds(row, width), pl.ds(d * LANES, LANES)] = grad[
                        d * width : (d + 1) * width, half * LANES : (half + 1) * LANES
                    ]
        part = pl.ds(k * group * width, group * width)
        copy = pltpu.make_async_copy(buf_ref.at[part], g_ref.at[part], sem_ref.at[k])
        copy.start()
        copies.append(copy)
    bias_ref[...] = jnp.broadcast_to(total, bias_ref.shape)
    for copy in copies:
        copy.wait()


def stream(hbm_ref, buf_ref, sem_ref, pieces):
    rows = buf_ref.shape[0] // pieces
    out = []
    for k in range(pieces):
        part = pl.ds(k * rows, rows)
        copy = pltpu.make_async_copy(hbm_ref.at[part], buf_ref.at[part], sem_ref.at[k])
        copy.start()
        out.append((part, copy))
    return out


def left_grad_kernel(scale, pieces, r_ref, g_ref, out_ref, panel_ref, buf_ref, pad_ref, sem_ref):
    copies = stream(g_ref, buf_ref, sem_ref, pieces)
    panel = jnp.swapaxes(r_ref[...].astype(F32), 0, 1).astype(BF)
    panel_ref[...] = panel
    for d in range(panel.shape[0]):
        pad_ref[pl.ds(d * LANES, LANES)] = padded_rows(panel[d], LANES)
    for part, copy in copies:
        copy.wait()
        out_ref[part] = (
            jnp.dot(buf_ref[part], pad_ref[...], preferred_element_type=F32) * scale
        ).astype(out_ref.dtype)


def right_grad_kernel(pieces, l_ref, g_ref, out_ref, buf_ref, acc_ref, block_ref, sem_ref):
    copies = stream(g_ref, buf_ref, sem_ref, pieces)
    chunk = 512
    for k, (part, copy) in enumerate(copies):
        lt = l_ref[part].T
        copy.wait()
        for n in range(acc_ref.shape[1] // chunk):
            lanes = pl.ds(n * chunk, chunk)
            term = jnp.dot(lt, buf_ref[part, lanes], preferred_element_type=F32)
            acc_ref[:, lanes] = term if k == 0 else acc_ref[:, lanes] + term
    columns, depth = out_ref.shape[:2]
    group = 8
    for first in range(0, depth, group):
        blocks = [
            acc_ref[:, d * LANES : (d + 1) * LANES].T[:columns]
            for d in range(first, first + group)
        ]
        block_ref[:, pl.ds(first, group)] = jnp.swapaxes(jnp.stack(blocks), 0, 1)
    out_ref[...] = block_ref[...].astype(out_ref.dtype)


def pair_kernel(
    width, group, l_ref, r_ref, t_ref, w_ref, off_ref, p_ref, pack_ref, gw_ref, wt_ref, rt_ref,
    outer_ref,
):
    columns = t_ref.shape[1]
    depth = r_ref.shape[0]

    @pl.when(pl.program_id(0) == 0)
    def _():
        gw_ref[...] = jnp.zeros_like(gw_ref)
        for n in range(w_ref.shape[0] // LANES):
            part = pl.ds(n * LANES, LANES)
            wt_ref[:, part] = w_ref[part].T
        for d in range(depth):
            rt_ref[:, pl.ds(d * LANES, LANES)] = padded_rows(r_ref[d], LANES).T

    per = 4
    for n in range(depth // per):
        block = jnp.dot(
            l_ref[...], rt_ref[:, pl.ds(n * per * LANES, per * LANES)], preferred_element_type=F32
        ).astype(BF)
        for i in range(group):
            for d in range(per):
                outer_ref[pl.ds((n * per + d) * width, width), pl.ds(i * LANES, LANES)] = block[
                    i * width : (i + 1) * width, d * LANES : (d + 1) * LANES
                ]
    offset = off_ref[...]
    out = jnp.dot(wt_ref[...], outer_ref[...], preferred_element_type=F32)
    for i in range(group):
        p_ref[i] = (out[:, i * LANES : (i + 1) * LANES].T[:columns] + offset).astype(BF)
    cotangent = jnp.concatenate([padded_rows(t_ref[i], LANES) for i in range(group)], axis=0)
    step = 256
    for n in range(gw_ref.shape[0] // step):
        part = pl.ds(n * step, step)
        gw_ref[part] += jnp.dot(outer_ref[part], cotangent, preferred_element_type=F32)

    @pl.when(pl.program_id(0) == pl.num_programs(0) - 1)
    def _():
        blocks, pack, out = pack_ref.shape
        main = gw_ref.shape[0] // blocks
        for n in range(blocks):
            block = padded_rows(gw_ref[pl.ds(n * main, main)], pack)
            pack_ref[n] = block.astype(BF)


def params():
    return pltpu.CompilerParams(
        dimension_semantics=("arbitrary",), vmem_limit_bytes=VMEM
    )


def outer_grads(cotangent, weight, width):
    rows, columns, out = cotangent.shape
    pieces = 10
    channels = weight.shape[0] * weight.shape[1]
    depth = channels // width
    return pl.pallas_call(
        functools.partial(outer_grad_kernel, width, pieces),
        in_specs=[pl.BlockSpec(memory_space=pltpu.VMEM)] * 2,
        out_specs=[
            pl.BlockSpec(memory_space=pl.ANY),
            pl.BlockSpec(memory_space=pltpu.VMEM),
            pl.BlockSpec(memory_space=pltpu.VMEM),
        ],
        out_shape=[
            jax.ShapeDtypeStruct((rows * width, depth * LANES), BF),
            jax.ShapeDtypeStruct((8, out), F32),
            jax.ShapeDtypeStruct((channels, out), BF),
        ],
        scratch_shapes=[
            pltpu.VMEM((rows * width, depth * LANES), BF),
            pltpu.SemaphoreType.DMA((pieces,)),
        ],
        compiler_params=pltpu.CompilerParams(vmem_limit_bytes=VMEM),
        cost_estimate=pl.CostEstimate(
            flops=4 * rows * columns * channels * out, bytes_accessed=22 << 20, transcendentals=0
        ),
        name="outer_grads",
    )(cotangent, weight)


def left_grads(right, grad, scale):
    rows, depth = grad.shape
    sequences = right.shape[2]
    pieces = 10
    return pl.pallas_call(
        functools.partial(left_grad_kernel, scale, pieces),
        in_specs=[
            pl.BlockSpec(memory_space=pltpu.VMEM),
            pl.BlockSpec(memory_space=pl.ANY),
        ],
        out_specs=[pl.BlockSpec(memory_space=pltpu.VMEM)] * 2,
        out_shape=[
            jax.ShapeDtypeStruct((rows, sequences), BF),
            jax.ShapeDtypeStruct((right.shape[1], right.shape[0], sequences), BF),
        ],
        scratch_shapes=[
            pltpu.VMEM((rows, depth), BF),
            pltpu.VMEM((depth, sequences), BF),
            pltpu.SemaphoreType.DMA((pieces,)),
        ],
        compiler_params=pltpu.CompilerParams(vmem_limit_bytes=VMEM),
        cost_estimate=pl.CostEstimate(
            flops=4 * rows * depth * sequences, bytes_accessed=22 << 20, transcendentals=0
        ),
        name="left_grads",
    )(right, grad)


def right_grads(left, grad, columns):
    rows, sequences = left.shape
    depth = grad.shape[1]
    pieces = 10
    return pl.pallas_call(
        functools.partial(right_grad_kernel, pieces),
        in_specs=[
            pl.BlockSpec(memory_space=pltpu.VMEM),
            pl.BlockSpec(memory_space=pl.ANY),
        ],
        out_specs=pl.BlockSpec(memory_space=pltpu.VMEM),
        out_shape=jax.ShapeDtypeStruct((columns, depth // LANES, sequences), BF),
        scratch_shapes=[
            pltpu.VMEM((rows, depth), BF),
            pltpu.VMEM((sequences, depth), F32),
            pltpu.VMEM((columns, depth // LANES, sequences), F32),
            pltpu.SemaphoreType.DMA((pieces,)),
        ],
        compiler_params=pltpu.CompilerParams(vmem_limit_bytes=VMEM),
        cost_estimate=pl.CostEstimate(
            flops=4 * rows * depth * sequences, bytes_accessed=22 << 20, transcendentals=0
        ),
        name="right_grads",
    )(left, grad)


def pairs(left, right, cotangent, weight, offset, width, blocks, pack):
    rows, columns, out = cotangent.shape
    sequences = left.shape[1]
    channels = weight.shape[0]
    group = 20
    depth = right.shape[0]
    return pl.pallas_call(
        functools.partial(pair_kernel, width, group),
        grid=(rows // group,),
        in_specs=[
            pl.BlockSpec((group * width, sequences), lambda i: (i, 0)),
            pl.BlockSpec(right.shape, lambda i: (0, 0, 0)),
            pl.BlockSpec((group, columns, out), lambda i: (i, 0, 0)),
            pl.BlockSpec((channels, out), lambda i: (0, 0)),
            pl.BlockSpec((1, out), lambda i: (0, 0)),
        ],
        out_specs=[
            pl.BlockSpec((group, columns, out), lambda i: (i, 0, 0)),
            pl.BlockSpec((blocks, pack, out), lambda i: (0, 0, 0)),
        ],
        out_shape=[
            jax.ShapeDtypeStruct((rows, columns, out), BF),
            jax.ShapeDtypeStruct((blocks, pack, out), BF),
        ],
        scratch_shapes=[
            pltpu.VMEM((channels, out), F32),
            pltpu.VMEM((out, channels), BF),
            pltpu.VMEM((sequences, depth * LANES), BF),
            pltpu.VMEM((channels, group * LANES), BF),
        ],
        compiler_params=params(),
        cost_estimate=pl.CostEstimate(
            flops=12 * rows * LANES * channels * out, bytes_accessed=6 << 20, transcendentals=0
        ),
        name="pairs",
    )(left, right, cotangent, weight, offset)


def after(value, *others):
    return lax.optimization_barrier((value, *others))[0]


def shards(
    sequence_features,
    first_projection,
    second_projection,
    final_projection,
    final_offset,
    edge_change_cotangent,
):
    n_row = lax.axis_size("row")
    n_col = lax.axis_size("col")
    owned, _, sequences = sequence_features.shape
    rows, columns, out = edge_change_cotangent.shape
    width = first_projection.shape[1]
    scale = 1.0 / sequences

    channels = final_projection.shape[0]
    weight = final_projection.reshape(width, width, out)
    offset = final_offset.reshape(1, out)

    left, right = project(
        sequence_features, first_projection.T, second_projection.T, scale, n_col
    )
    right = swap_axes(right)
    grad, bias_local, weight = outer_grads(
        edge_change_cotangent, after(weight, left), width
    )
    left = exchange(left, "col").reshape(rows * width, sequences)

    right = gather_blocks(after(right, bias_local), "row").reshape(columns, width, sequences)

    right_part = right_grads(left, grad, columns)
    left_part, panel = left_grads(after(right, right_part), grad, scale)
    right_sum = scatter_blocks(right_part, "row")

    each = width // n_row
    main = channels // n_row
    pack = -(-(main + each + 1) // 8) * 8
    pair_delta, total = pairs(
        left, panel, edge_change_cotangent, weight, after(offset, left_part, right_sum), width,
        n_row, pack,
    )
    left_sum = scatter_blocks(left_part.reshape(rows, width, sequences), "col")

    exact = lax.Precision.HIGHEST
    left_weight = jnp.einsum(
        "gph,gah->ap", sequence_features.astype(F32), left_sum, precision=exact
    )
    right_back = swap_axes(right_sum)
    right_weight = jnp.einsum(
        "gph,gah->ap", sequence_features.astype(F32), right_back, precision=exact
    )

    small = jnp.concatenate([left_weight, right_weight], axis=1).reshape(n_row, each, LANES)
    bias = jnp.pad(bias_local[:1][None], ((0, n_row - 1), (0, 0), (0, 0)))
    small = jnp.concatenate([small, bias], axis=1).astype(BF)
    total = total + jnp.pad(small, ((0, 0), (main, pack - main - each - 1), (0, 0)))
    total = scatter_blocks(total.reshape(n_row * pack, out), "row").astype(BF)
    alignment_gradient = jnp.einsum(
        "awr,iw->air", left_sum, first_projection.astype(F32), precision=exact
    ) + jnp.einsum("awr,iw->air", right_back, second_projection.astype(F32), precision=exact)
    total = jnp.sum(gather_blocks(total, "col").astype(F32), axis=0).astype(BF)
    total = gather_blocks(total, "row")
    total, left_weight, right_weight, bias = unpack(
        total, width, left_weight.shape[1], 1.0 / (owned * n_row * n_col)
    )
    return (
        pair_delta,
        alignment_gradient,
        left_weight.T,
        right_weight.T,
        total.reshape(channels, out),
        bias.reshape(out),
    )


def solution(mesh):
    placed = (P(("row", "col"), None, None), P(), P(), P(), P(), P("row", "col", None))
    return jax.shard_map(
        shards,
        mesh=mesh,
        in_specs=placed,
        out_specs=(P("row", "col", None), P(("row", "col"), None, None), P(), P(), P(), P()),
        check_vma=False,
    )
```

```python
import functools

import jax
import jax.numpy as jnp
from jax import lax
from jax.experimental import pallas as pl
from jax.experimental.pallas import tpu as pltpu
from jax.sharding import PartitionSpec as P

BF = jnp.bfloat16
F32 = jnp.float32
LANES = 128
VMEM = 56 * 1024 * 1024
STREAM = 44 * 1024 * 1024


def exchange(x, axis):
    return lax.all_to_all(x, axis, 0, 0, tiled=True)


def gather_blocks(x, axis):
    return exchange(jnp.broadcast_to(x[None], (lax.axis_size(axis), *x.shape)), axis)


def scatter_blocks(x, axis):
    n = lax.axis_size(axis)
    x = exchange(x.reshape(n, x.shape[0] // n, *x.shape[1:]), axis)
    return jnp.sum(x.astype(F32), axis=0)


def swap_axes(x):
    n = lax.axis_size("row")
    return lax.ppermute(
        x, ("row", "col"), [(r * n + c, c * n + r) for r in range(n) for c in range(n)]
    )


def project_kernel(scale, x_ref, first_ref, second_ref, left_ref, right_ref):
    for n in range(x_ref.shape[0]):
        x = x_ref[n]
        left = jnp.dot(first_ref[...], x, preferred_element_type=F32).astype(BF)
        left = (left.astype(F32) * scale).astype(BF)
        for copy in range(left_ref.shape[0]):
            left_ref[copy, n] = left
        right_ref[n] = jnp.dot(second_ref[...], x, preferred_element_type=F32).astype(BF)


def project(source, first, second, scale, copies):
    owned, _, sequences = source.shape
    width = first.shape[0]
    return pl.pallas_call(
        functools.partial(project_kernel, scale),
        out_shape=[
            jax.ShapeDtypeStruct((copies, owned, width, sequences), BF),
            jax.ShapeDtypeStruct((owned, width, sequences), BF),
        ],
        compiler_params=pltpu.CompilerParams(vmem_limit_bytes=VMEM),
        cost_estimate=pl.CostEstimate(flops=1 << 22, bytes_accessed=1 << 20, transcendentals=0),
        name="project",
    )(source, first, second)


def unpack_kernel(inverse, pack_ref, weight_ref, left_ref, right_ref, bias_ref):
    width = weight_ref.shape[0]
    blocks = pack_ref.shape[0]
    main = weight_ref.shape[0] * weight_ref.shape[1] // blocks
    each = width // blocks
    total = [pack_ref[n] * inverse for n in range(blocks)]
    weight = jnp.concatenate([t[:main] for t in total], axis=0).reshape(weight_ref.shape)
    weight_ref[...] = jnp.swapaxes(weight, 0, 1)
    half = left_ref.shape[1]
    for n in range(blocks):
        rows = total[n][main : main + each]
        left_ref[pl.ds(n * each, each)] = rows[:, :half]
        right_ref[pl.ds(n * each, each)] = rows[:, half:]
    bias_ref[...] = total[0][main + each : main + each + 1]


def unpack(packed, width, half, inverse):
    out = packed.shape[2]
    return pl.pallas_call(
        functools.partial(unpack_kernel, inverse),
        out_shape=[
            jax.ShapeDtypeStruct((width, width, out), F32),
            jax.ShapeDtypeStruct((width, half), F32),
            jax.ShapeDtypeStruct((width, half), F32),
            jax.ShapeDtypeStruct((1, out), F32),
        ],
        compiler_params=pltpu.CompilerParams(vmem_limit_bytes=16 << 20),
        cost_estimate=pl.CostEstimate(flops=1 << 20, bytes_accessed=1 << 20, transcendentals=0),
        name="unpack",
    )(packed)


def padded_rows(t, rows):
    return jnp.concatenate([t, jnp.zeros((rows - t.shape[0], t.shape[1]), t.dtype)], axis=0)


def outer_grad_kernel(
    width, pieces, t_ref, natural_ref, g_ref, bias_ref, w_ref, buf_ref, sem_ref
):
    channels = w_ref.shape[0]
    swapped = jnp.swapaxes(natural_ref[...].astype(F32), 0, 1)
    w_ref[...] = swapped.reshape(w_ref.shape).astype(BF)
    group = t_ref.shape[0] // pieces
    total = jnp.zeros((1, LANES), F32)
    copies = []
    for k in range(pieces):
        for first in range(k * group, (k + 1) * group, 2):
            a, b = t_ref[first], t_ref[first + 1]
            total = total + jnp.sum(a.astype(F32) + b.astype(F32), axis=0, keepdims=True)
            both = jnp.concatenate([padded_rows(a, LANES), padded_rows(b, LANES)], axis=0)
            grad = lax.dot_general(
                w_ref[...], both, (((1,), (1,)), ((), ())), preferred_element_type=F32
            ).astype(BF)
            for half in range(2):
                row = (first + half) * width
                for d in range(channels // width):
                    buf_ref[pl.ds(row, width), pl.ds(d * LANES, LANES)] = grad[
                        d * width : (d + 1) * width, half * LANES : (half + 1) * LANES
                    ]
        part = pl.ds(k * group * width, group * width)
        copy = pltpu.make_async_copy(buf_ref.at[part], g_ref.at[part], sem_ref.at[k])
        copy.start()
        copies.append(copy)
    bias_ref[...] = jnp.broadcast_to(total, bias_ref.shape)
    for copy in copies:
        copy.wait()


def stream(hbm_ref, buf_ref, sem_ref, pieces):
    rows = buf_ref.shape[0] // pieces
    out = []
    for k in range(pieces):
        part = pl.ds(k * rows, rows)
        copy = pltpu.make_async_copy(hbm_ref.at[part], buf_ref.at[part], sem_ref.at[k])
        copy.start()
        out.append((part, copy))
    return out


def left_grad_kernel(scale, pieces, r_ref, g_ref, out_ref, panel_ref, buf_ref, pad_ref, sem_ref):
    copies = stream(g_ref, buf_ref, sem_ref, pieces)
    panel = jnp.swapaxes(r_ref[...].astype(F32), 0, 1).astype(BF)
    panel_ref[...] = panel
    for d in range(panel.shape[0]):
        pad_ref[pl.ds(d * LANES, LANES)] = padded_rows(panel[d], LANES)
    for part, copy in copies:
        copy.wait()
        out_ref[part] = (
            jnp.dot(buf_ref[part], pad_ref[...], preferred_element_type=F32) * scale
        ).astype(out_ref.dtype)


def right_grad_kernel(pieces, l_ref, g_ref, out_ref, buf_ref, acc_ref, block_ref, sem_ref):
    copies = stream(g_ref, buf_ref, sem_ref, pieces)
    chunk = 512
    for k, (part, copy) in enumerate(copies):
        lt = l_ref[part].T
        copy.wait()
        for n in range(acc_ref.shape[1] // chunk):
            lanes = pl.ds(n * chunk, chunk)
            term = jnp.dot(lt, buf_ref[part, lanes], preferred_element_type=F32)
            acc_ref[:, lanes] = term if k == 0 else acc_ref[:, lanes] + term
    columns, depth = out_ref.shape[:2]
    group = 8
    for first in range(0, depth, group):
        blocks = [
            acc_ref[:, d * LANES : (d + 1) * LANES].T[:columns]
            for d in range(first, first + group)
        ]
        block_ref[:, pl.ds(first, group)] = jnp.swapaxes(jnp.stack(blocks), 0, 1)
    out_ref[...] = block_ref[...].astype(out_ref.dtype)


def pair_kernel(
    width, group, l_ref, r_ref, t_ref, w_ref, off_ref, p_ref, pack_ref, gw_ref, wt_ref, rt_ref,
    outer_ref,
):
    columns = t_ref.shape[1]
    depth = r_ref.shape[0]

    @pl.when(pl.program_id(0) == 0)
    def _():
        gw_ref[...] = jnp.zeros_like(gw_ref)
        for n in range(w_ref.shape[0] // LANES):
            part = pl.ds(n * LANES, LANES)
            wt_ref[:, part] = w_ref[part].T
        for d in range(depth):
            rt_ref[:, pl.ds(d * LANES, LANES)] = padded_rows(r_ref[d], LANES).T

    per = 4
    for n in range(depth // per):
        block = jnp.dot(
            l_ref[...], rt_ref[:, pl.ds(n * per * LANES, per * LANES)], preferred_element_type=F32
        ).astype(BF)
        for i in range(group):
            for d in range(per):
                outer_ref[pl.ds((n * per + d) * width, width), pl.ds(i * LANES, LANES)] = block[
                    i * width : (i + 1) * width, d * LANES : (d + 1) * LANES
                ]
    offset = off_ref[...]
    out = jnp.dot(wt_ref[...], outer_ref[...], preferred_element_type=F32)
    for i in range(group):
        p_ref[i] = (out[:, i * LANES : (i + 1) * LANES].T[:columns] + offset).astype(BF)
    cotangent = jnp.concatenate([padded_rows(t_ref[i], LANES) for i in range(group)], axis=0)
    step = 256
    for n in range(gw_ref.shape[0] // step):
        part = pl.ds(n * step, step)
        gw_ref[part] += jnp.dot(outer_ref[part], cotangent, preferred_element_type=F32)

    @pl.when(pl.program_id(0) == pl.num_programs(0) - 1)
    def _():
        pack_ref[...] = gw_ref[...].astype(BF)


def params():
    return pltpu.CompilerParams(
        dimension_semantics=("arbitrary",), vmem_limit_bytes=VMEM
    )


def outer_grads(cotangent, weight, width):
    rows, columns, out = cotangent.shape
    pieces = 10
    channels = weight.shape[0] * weight.shape[1]
    depth = channels // width
    return pl.pallas_call(
        functools.partial(outer_grad_kernel, width, pieces),
        in_specs=[pl.BlockSpec(memory_space=pltpu.VMEM)] * 2,
        out_specs=[
            pl.BlockSpec(memory_space=pl.ANY),
            pl.BlockSpec(memory_space=pltpu.VMEM),
            pl.BlockSpec(memory_space=pltpu.VMEM),
        ],
        out_shape=[
            jax.ShapeDtypeStruct((rows * width, depth * LANES), BF),
            jax.ShapeDtypeStruct((8, out), F32),
            jax.ShapeDtypeStruct((channels, out), BF),
        ],
        scratch_shapes=[
            pltpu.VMEM((rows * width, depth * LANES), BF),
            pltpu.SemaphoreType.DMA((pieces,)),
        ],
        compiler_params=pltpu.CompilerParams(vmem_limit_bytes=VMEM),
        cost_estimate=pl.CostEstimate(
            flops=4 * rows * columns * channels * out, bytes_accessed=22 << 20, transcendentals=0
        ),
        name="outer_grads",
    )(cotangent, weight)


def left_grads(right, grad, scale):
    rows, depth = grad.shape
    sequences = right.shape[2]
    pieces = 10
    return pl.pallas_call(
        functools.partial(left_grad_kernel, scale, pieces),
        in_specs=[
            pl.BlockSpec(memory_space=pltpu.VMEM),
            pl.BlockSpec(memory_space=pl.ANY),
        ],
        out_specs=[pl.BlockSpec(memory_space=pltpu.VMEM)] * 2,
        out_shape=[
            jax.ShapeDtypeStruct((rows, sequences), BF),
            jax.ShapeDtypeStruct((right.shape[1], right.shape[0], sequences), BF),
        ],
        scratch_shapes=[
            pltpu.VMEM((rows, depth), BF),
            pltpu.VMEM((depth, sequences), BF),
            pltpu.SemaphoreType.DMA((pieces,)),
        ],
        compiler_params=pltpu.CompilerParams(vmem_limit_bytes=STREAM),
        cost_estimate=pl.CostEstimate(
            flops=4 * rows * depth * sequences, bytes_accessed=22 << 20, transcendentals=0
        ),
        name="left_grads",
    )(right, grad)


def right_grads(left, grad, columns):
    rows, sequences = left.shape
    depth = grad.shape[1]
    pieces = 10
    return pl.pallas_call(
        functools.partial(right_grad_kernel, pieces),
        in_specs=[
            pl.BlockSpec(memory_space=pltpu.VMEM),
            pl.BlockSpec(memory_space=pl.ANY),
        ],
        out_specs=pl.BlockSpec(memory_space=pltpu.VMEM),
        out_shape=jax.ShapeDtypeStruct((columns, depth // LANES, sequences), BF),
        scratch_shapes=[
            pltpu.VMEM((rows, depth), BF),
            pltpu.VMEM((sequences, depth), F32),
            pltpu.VMEM((columns, depth // LANES, sequences), F32),
            pltpu.SemaphoreType.DMA((pieces,)),
        ],
        compiler_params=pltpu.CompilerParams(vmem_limit_bytes=STREAM),
        cost_estimate=pl.CostEstimate(
            flops=4 * rows * depth * sequences, bytes_accessed=22 << 20, transcendentals=0
        ),
        name="right_grads",
    )(left, grad)


def pairs(left, right, cotangent, weight, offset, width):
    rows, columns, out = cotangent.shape
    sequences = left.shape[1]
    channels = weight.shape[0]
    group = 20
    depth = right.shape[0]
    return pl.pallas_call(
        functools.partial(pair_kernel, width, group),
        grid=(rows // group,),
        in_specs=[
            pl.BlockSpec((group * width, sequences), lambda i: (i, 0)),
            pl.BlockSpec(right.shape, lambda i: (0, 0, 0)),
            pl.BlockSpec((group, columns, out), lambda i: (i, 0, 0)),
            pl.BlockSpec((channels, out), lambda i: (0, 0)),
            pl.BlockSpec((1, out), lambda i: (0, 0)),
        ],
        out_specs=[
            pl.BlockSpec((group, columns, out), lambda i: (i, 0, 0)),
            pl.BlockSpec((channels, out), lambda i: (0, 0)),
        ],
        out_shape=[
            jax.ShapeDtypeStruct((rows, columns, out), BF),
            jax.ShapeDtypeStruct((channels, out), BF),
        ],
        scratch_shapes=[
            pltpu.VMEM((channels, out), F32),
            pltpu.VMEM((out, channels), BF),
            pltpu.VMEM((sequences, depth * LANES), BF),
            pltpu.VMEM((channels, group * LANES), BF),
        ],
        compiler_params=params(),
        cost_estimate=pl.CostEstimate(
            flops=12 * rows * LANES * channels * out, bytes_accessed=6 << 20, transcendentals=0
        ),
        name="pairs",
    )(left, right, cotangent, weight, offset)


def after(value, *others):
    return lax.optimization_barrier((value, *others))[0]


def shards(
    sequence_features,
    first_projection,
    second_projection,
    final_projection,
    final_offset,
    edge_change_cotangent,
):
    n_row = lax.axis_size("row")
    n_col = lax.axis_size("col")
    owned, _, sequences = sequence_features.shape
    rows, columns, out = edge_change_cotangent.shape
    width = first_projection.shape[1]
    scale = 1.0 / sequences

    channels = final_projection.shape[0]
    weight = final_projection.reshape(width, width, out)
    offset = final_offset.reshape(1, out)

    left, right = project(
        sequence_features, first_projection.T, second_projection.T, scale, n_col
    )
    right = swap_axes(right)
    grad, bias_local, weight = outer_grads(
        edge_change_cotangent, after(weight, left), width
    )
    left = exchange(left, "col").reshape(rows * width, sequences)

    right = gather_blocks(after(right, bias_local), "row").reshape(columns, width, sequences)

    right_part = right_grads(left, grad, columns)
    left_part, panel = left_grads(after(right, right_part), grad, scale)
    right_sum = scatter_blocks(right_part, "row")

    each = width // n_row
    main = channels // n_row
    pack = -(-(main + each + 1) // 8) * 8
    pair_delta, total = pairs(
        left, panel, edge_change_cotangent, weight, after(offset, left_part, right_sum), width
    )
    left_sum = scatter_blocks(left_part.reshape(rows, width, sequences), "col")

    exact = lax.Precision.HIGHEST
    left_weight = jnp.einsum(
        "gph,gah->ap", sequence_features.astype(F32), left_sum, precision=exact
    )
    right_back = swap_axes(right_sum)
    right_weight = jnp.einsum(
        "gph,gah->ap", sequence_features.astype(F32), right_back, precision=exact
    )

    small = jnp.concatenate([left_weight, right_weight], axis=1).reshape(n_row, each, LANES)
    bias = jnp.pad(bias_local[:1][None], ((0, n_row - 1), (0, 0), (0, 0)))
    rest = jnp.zeros((n_row, pack - main - each - 1, out), F32)
    small = jnp.concatenate([small, bias, rest], axis=1).astype(BF)
    total = jnp.concatenate([total.reshape(n_row, main, out), small], axis=1)
    total = scatter_blocks(total.reshape(n_row * pack, out), "row").astype(BF)
    alignment_gradient = jnp.einsum(
        "awr,iw->air", left_sum, first_projection.astype(F32), precision=exact
    ) + jnp.einsum("awr,iw->air", right_back, second_projection.astype(F32), precision=exact)
    total = jnp.sum(gather_blocks(total, "col").astype(F32), axis=0).astype(BF)
    total = gather_blocks(total, "row").astype(F32)
    total, left_weight, right_weight, bias = unpack(
        total, width, left_weight.shape[1], 1.0 / (owned * n_row * n_col)
    )
    return (
        pair_delta,
        alignment_gradient,
        left_weight.T,
        right_weight.T,
        total.reshape(channels, out),
        bias.reshape(out),
    )


def solution(mesh):
    placed = (P(("row", "col"), None, None), P(), P(), P(), P(), P("row", "col", None))
    return jax.shard_map(
        shards,
        mesh=mesh,
        in_specs=placed,
        out_specs=(P("row", "col", None), P(("row", "col"), None, None), P(), P(), P(), P()),
        check_vma=False,
    )
```
